32 devices in a mesh: rows: 8 (over z, x), feat: 4 (over y, core).
Axes of the slice: x: 2, y: 2, z: 4, core: 2. Of those that a mesh axis runs over, the one named last changes fastest.
Arguments:
- features: float32 [8192, 512], P('rows', 'feat')
- counts: int32 [8], P('rows'), may hold values from 256 to 1024, as said below
- validity: int32 [8192], P('rows'), may hold values from 0 to 1, as said below
- mask_logits: float32 [6, 512], P(None, 'feat'), may hold values from -4 to 4
- w_update: float32 [6, 1024, 512], P(None, None, 'feat'), may hold values from -0.1875 to 0.1875
- w_reset: float32 [6, 1024, 512], P(None, None, 'feat'), may hold values from -0.1875 to 0.1875
- w_candidate: float32 [6, 1024, 512], P(None, None, 'feat'), may hold values from -0.1875 to 0.1875
- b_update: float32 [6, 512], P(None, 'feat'), may hold values from -3 to 3
- b_reset: float32 [6, 512], P(None, 'feat'), may hold values from -3 to 3
- b_candidate: float32 [6, 512], P(None, 'feat'), may hold values from -3 to 3
- norm_gain: float32 [512], P('feat'), may hold values from 0.5 to 1.5
- norm_shift: float32 [512], P('feat'), may hold values from -3 to 3
- w_head: float32 [512, 256], P('feat'), may hold values from -0.25 to 0.25
- b_head: float32 [256], replicated, may hold values from -3 to 3
- w_out: float32 [256, 10], replicated, may hold values from -0.75 to 0.75
- b_out: float32 [10], replicated, may hold values from -3 to 3
- cotangent: float32 [8192, 10], P('rows'), may hold values from -6 to 6
Outputs:
- logits: float32 [8192, 10], P('rows')
- grad_features: float32 [8192, 512], P('rows', 'feat')
- grad_mask: float32 [6, 512], P(None, 'feat')
- grad_w_update: float32 [6, 1024, 512], P(None, None, 'feat')
- grad_w_reset: float32 [6, 1024, 512], P(None, None, 'feat')
- grad_w_candidate: float32 [6, 1024, 512], P(None, None, 'feat')
- grad_b_update: float32 [6, 512], P(None, 'feat')
- grad_b_reset: float32 [6, 512], P(None, 'feat')
- grad_b_candidate: float32 [6, 512], P(None, 'feat')
- grad_norm_gain: float32 [512], P('feat')
- grad_norm_shift: float32 [512], P('feat')
- grad_w_head: float32 [512, 256], P('feat')
- grad_b_head: float32 [256], replicated
- grad_w_out: float32 [256, 10], replicated
- grad_b_out: float32 [10], replicated
The draws below stay inside these ranges and needn't reach their ends.
Inputs may be any that keep to these rules, and one draw needn't show every extreme that they name: Device d of the rows axis has counts[d] filled rows at the start of its block of 1024 rows, the rest being padding; in every draw some device is full. `validity`: the first row of each device's block of 1024 rows is 1.
All inputs are finite; a program needn't handle non-finite values.
Results may differ from the reference program's by a relative error of at most 0.0003.
Values sent between devices are 32-bit elements; how exact they have to be, the bound alone decides.
A program may use at most 192 MiB of HBM per device.

```python
import jax
import jax.numpy as jnp
from jax import lax

D = 512
HID = 256
CLASSES = 10
SECTIONS = 6
CAP = 1024
ROWS = 8192


def draw_features(key, part):
    key = jax.random.fold_in(key, 3)
    return jax.random.normal(key, (ROWS, D), jnp.float32)


def draw_counts(key, part):
    key = jax.random.fold_in(key, 7)
    first_key, second_key = jax.random.split(key)
    groups = ROWS // CAP
    lowest = CAP // 4
    slot_index = jnp.arange(groups, dtype=jnp.int32)
    ramp_base = lowest + (CAP - lowest) * slot_index // max(groups - 1, 1)
    jitter = jax.random.randint(first_key, (groups,), -(CAP // 8), CAP // 8 + 1, dtype=jnp.int32)
    filled = jnp.clip(ramp_base + jitter, lowest, CAP)
    chosen = jax.random.randint(second_key, (), groups - max(groups // 4, 1), groups, dtype=jnp.int32)
    return jnp.where(slot_index == chosen, CAP, filled).astype(jnp.int32)


def draw_validity(key, part):
    key = jax.random.fold_in(key, 11)
    drop_picks = jax.random.randint(key, (ROWS,), 0, 4, dtype=jnp.int32)
    leading = jnp.arange(ROWS, dtype=jnp.int32) % CAP == 0
    return jnp.where(leading | (drop_picks != 0), 1, 0).astype(jnp.int32)


def levels(rng, dims, shards, smallest, largest):
    def one(dim, blocks):
        heights = jax.random.uniform(jax.random.fold_in(jax.random.fold_in(rng, 6), dim), (blocks,), jnp.float32, smallest / len(shards), largest / len(shards))
        return jnp.repeat(jnp.exp(heights), dims[dim] // blocks).reshape((-1,) + (1,) * (len(dims) - dim - 1))

    factor_of = one(*shards[0])
    for cut in shards[1:]:
        factor_of = factor_of * one(*cut)
    return factor_of


def centred(key, extent, spread, limit, cuts=(), held_as=jnp.bfloat16):
    array = jax.random.normal(key, extent, jnp.float32) * spread
    if len(cuts) > 0:
        array = levels(key, extent, cuts, -0.22, 0.18) * array
    return jnp.clip(array, min=-limit, max=limit).astype(held_as)


def setup_inputs(seed: int = 0) -> dict:
    arg_keys = jax.random.split(jax.random.key(seed), 18)
    features = draw_features(jax.random.fold_in(arg_keys[17], 71), 0)
    counts = draw_counts(jax.random.fold_in(arg_keys[17], 71), 0)
    validity = draw_validity(jax.random.fold_in(arg_keys[17], 71), 0)
    mask_logits = centred(arg_keys[3], (SECTIONS, D), 1.0, 4.0, ((1, 4),), jnp.float32)
    w_update = centred(arg_keys[4], (SECTIONS, 2 * D, D), (2 * D) ** -0.5, 0.1875, ((2, 4),), jnp.float32)
    w_reset = centred(arg_keys[5], (SECTIONS, 2 * D, D), (2 * D) ** -0.5, 0.1875, ((2, 4),), jnp.float32)
    w_candidate = centred(arg_keys[6], (SECTIONS, 2 * D, D), (2 * D) ** -0.5, 0.1875, ((2, 4),), jnp.float32)
    b_update = centred(arg_keys[7], (SECTIONS, D), 0.5, 3.0, ((1, 4),), jnp.float32)
    b_reset = centred(arg_keys[8], (SECTIONS, D), 0.5, 3.0, ((1, 4),), jnp.float32)
    b_candidate = centred(arg_keys[9], (SECTIONS, D), 0.5, 3.0, ((1, 4),), jnp.float32)
    norm_gain = jnp.clip(0.5 + 1.0 * jax.random.uniform(arg_keys[10], (D,), jnp.float32) ** levels(arg_keys[10], (D,), ((0, 4),), -0.2, 0.2), 0.5, 1.5)
    norm_shift = centred(arg_keys[11], (D,), 0.5, 3.0, ((0, 4),), jnp.float32)
    w_head = centred(arg_keys[12], (D, HID), D ** -0.5, 0.25, ((0, 4),), jnp.float32)
    b_head = centred(arg_keys[13], (HID,), 0.5, 3.0, (), jnp.float32)
    w_out = centred(arg_keys[14], (HID, CLASSES), (HID // 4) ** -0.5, 0.75, (), jnp.float32)
    b_out = centred(arg_keys[15], (CLASSES,), 0.5, 3.0, (), jnp.float32)
    cotangent = centred(arg_keys[16], (ROWS, CLASSES), 1.0, 6.0, ((0, 8),), jnp.float32)
    return {"features": features, "counts": counts, "validity": validity, "mask_logits": mask_logits, "w_update": w_update, "w_reset": w_reset, "w_candidate": w_candidate, "b_update": b_update, "b_reset": b_reset, "b_candidate": b_candidate, "norm_gain": norm_gain, "norm_shift": norm_shift, "w_head": w_head, "b_head": b_head, "w_out": w_out, "b_out": b_out, "cotangent": cotangent}


@jax.custom_vjp
def low(v):
    return lax.optimization_barrier(v.astype(jnp.bfloat16)).astype(jnp.float32)

@jax.custom_vjp
def low_back(v):
    return v

def low_keep(v):
    return (low(v), None)

def low_pass(kept, grad):
    return (grad,)

def back_keep(v):
    return (v, None)

def back_low(kept, grad):
    return (low(grad),)
low.defvjp(low_keep, low_pass)
low_back.defvjp(back_keep, back_low)

def matmul(left_side, right_side):
    return jnp.dot(left_side, right_side, precision=lax.Precision.HIGHEST, preferred_element_type=jnp.float32)

def reference(features, counts, validity, mask_logits, w_update, w_reset, w_candidate, b_update, b_reset, b_candidate, norm_gain, norm_shift, w_head, b_head, w_out, b_out, cotangent):
    position = jnp.arange(ROWS)
    device_of = position // CAP
    filled = (position % CAP < counts[device_of]).astype(jnp.float32)
    weight = filled * validity.astype(jnp.float32)
    column = weight[:, None]

    def forward(features, mask_logits, w_update, w_reset, w_candidate, b_update, b_reset, b_candidate, norm_gain, norm_shift, w_head, b_head, w_out, b_out):
        current = features
        for section_num in range(SECTIONS):
            scaled = features * (D * jax.nn.softmax(mask_logits[section_num]))
            upper = jnp.concatenate([current, scaled], 1)
            update = jax.nn.sigmoid(matmul(upper, w_update[section_num]) + b_update[section_num])
            resets = jax.nn.sigmoid(matmul(upper, w_reset[section_num]) + b_reset[section_num])
            lower = jnp.concatenate([resets * current, scaled], 1)
            candidate = jnp.tanh(matmul(lower, w_candidate[section_num]) + b_candidate[section_num])
            current = current + update * (candidate - current)
        count_all = jnp.sum(weight)
        col_mean = lax.optimization_barrier(jnp.sum(column * current, 0)) / count_all
        centered = current - col_mean
        variance = lax.optimization_barrier(jnp.sum(column * centered * centered, 0)) / count_all
        normed = centered * lax.rsqrt(variance + 1e-05) * norm_gain + norm_shift
        hidden = jax.nn.gelu(matmul(normed, w_head) + b_head, approximate=False)
        return (matmul(hidden, w_out) + b_out) * column
    logits, pullback = jax.vjp(forward, features, mask_logits, w_update, w_reset, w_candidate, b_update, b_reset, b_candidate, norm_gain, norm_shift, w_head, b_head, w_out, b_out)
    gradients = pullback(cotangent)
    return (logits, gradients[0], gradients[1], gradients[2], gradients[3], gradients[4], gradients[5], gradients[6], gradients[7], gradients[8], gradients[9], gradients[10], gradients[11], gradients[12], gradients[13])
```

```python
import functools

import jax
import jax.numpy as jnp
from jax import lax
from jax.experimental import pallas as pl
from jax.experimental.pallas import tpu as pltpu
from jax.sharding import PartitionSpec as P

MESH = pl.DeviceIdType.MESH
F32, BF16 = jnp.float32, jnp.bfloat16
LANES = 128
PAR = 32
TALL = 16
CUTS = 2
SLOTS = 3 * CUTS


def schedule(levels):
    sums = [1, 4, 6, 8] + [8 + k for k in range(1, levels - 1)]
    gap = 2 if levels < 4 else 1
    return sums + [sums[-1] + 1 + gap * k for k in range(levels)]


def rings(levels):
    return -(-(schedule(levels)[levels + 2] + 1) // SLOTS), 2


def flip(index, stride):
    return index + stride - 2 * stride * ((index // stride) % 2)


def split(value):
    high = value.astype(BF16)
    return high, (value - high.astype(F32)).astype(BF16)


def dot3(left, right, dims):
    def one(a, b):
        return lax.dot_general(a, b, (dims, ((), ())), preferred_element_type=F32)

    return one(left[0], right[1]) + one(left[1], right[0]) + one(left[0], right[0])


NN, NT, TN = ((1,), (0,)), ((1,), (1,)), ((0,), (0,))


def remote(src, dst, send, recv, device):
    return pltpu.make_async_remote_copy(
        src_ref=src, dst_ref=dst, send_sem=send, recv_sem=recv, device_id=device, device_id_type=MESH
    )


def meet(devices):
    barrier = pltpu.get_barrier_semaphore()
    for device in devices:
        pl.semaphore_signal(barrier, inc=1, device_id=device, device_id_type=MESH)
    pl.semaphore_wait(barrier, len(devices))


def sum_slots(ref):
    total = ref[0]
    for k in range(1, ref.shape[0]):
        total = total + ref[k]
    return total


def merge_stats(ref):
    parts = [ref[k] for k in range(ref.shape[0])]
    count = functools.reduce(jnp.add, [p[0:1] for p in parts])
    sums = functools.reduce(jnp.add, [p[1:2] for p in parts])
    mean = sums / jnp.maximum(count, 1.0)
    square = jnp.zeros_like(sums)
    for p in parts:
        gap = p[1:2] / jnp.maximum(p[0:1], 1.0) - mean
        square = square + (p[2:3] + p[0:1] * gap * gap)
    return jnp.concatenate([count, sums, square, jnp.zeros((5, sums.shape[1]), F32)], axis=0)


def kernel(
    sections, rows, levels, classes,
    feat_ref, wz_ref, wr_ref, wo_ref, whead_ref, count_ref, valid_ref,
    mask_ref, bz_ref, br_ref, bo_ref, gain_ref, shift_ref, bhead_ref, wout_ref, bout_ref, cot_ref,
    gz_out, gr_out, go_out, gfeat_out, ghead_out, logit_out, tiny_out, vec_out, wfull,
    x_buf, small_buf, par, hs, zs, rs, cs, weight, upper,
    whead, x_hat, logit_buf, dh, d_in, d_reset, gin, vec,
    small_ref, wout_buf, dlog_buf, turn,
    grads, core_buf, total, land,
    h_grads, h_core, h_total, h_land,
    ex_a, ex_a_feat, ex_a_rows, ex_b, ex_b_feat, ex_b_rows, ex_c_feat, ex_c_rows,
    first_s, first_r, first_l, fy_s, fy_r, a_s, a_r, x_s, x_r, z_s, z_r, b_s, b_r, c_s, c_r,
    own_s, own_r, far_s, far_r, load_w, logit_s, logit_r, gf_s, gf_r, gf_l,
    ef_s, ef_r, er_s, er_r,
    core_s, core_r, rs_s, rs_r, ag_s, ag_r, out_l, hu_s, hu_r, hu_l,
):
    r, f = lax.axis_index("rows"), lax.axis_index("feat")
    weights = (wz_ref, wr_ref, wo_ref)
    units = 3 * sections
    depth = wz_ref.shape[1]
    mine, width = x_buf.shape
    blocks = small_buf.shape[0]
    half = width // 2
    core, far, both = flip(f, 1), flip(f, 2), flip(flip(f, 1), 2)
    others = (core, far, both)
    rx, rz = flip(r, 1), flip(r, 2)
    quarter = depth // 4
    cut_b, cut_c = 3 * quarter // 8, 3 * quarter // 8 + 5 * quarter // 16
    q = 2 * (r % 2) + (r // 2) % 2
    q_x, q_z, q_d = flip(q, 2), flip(q, 1), flip(flip(q, 1), 2)

    def lanes(index):
        return pl.ds(pl.multiple_of(index * LANES, LANES), LANES)

    def part(start, size):
        return pl.ds(pl.multiple_of(start, 8), size)

    def rows_of(index, start, size):
        return part(index * quarter + start, size)

    meet([(r, peer) for peer in others] + [(lax.rem(r + k, rows), f) for k in range(1, rows)])

    small_ref[...] = jnp.zeros_like(small_ref)
    for k, ref in enumerate((mask_ref, bz_ref, br_ref, bo_ref)):
        small_ref[k * sections : (k + 1) * sections] = ref[...]
    small_ref[4 * sections : 4 * sections + 1] = gain_ref[...]
    small_ref[4 * sections + 1 : 4 * sections + 2] = shift_ref[...]
    own_rows = pl.ds(pl.multiple_of(f * mine, mine), mine)
    firsts, heads = [], []
    for k, peer in enumerate(others):
        chunk = pl.ds(pl.multiple_of(peer * mine, mine), mine)
        firsts += [
            remote(small_ref, small_buf.at[f], first_s.at[k], first_r.at[k], (r, peer)),
            remote(feat_ref.at[chunk], x_buf.at[:, lanes(f)], first_s.at[3 + k], first_r.at[3 + k], (r, peer)),
        ]
        heads.append(remote(whead_ref, whead.at[lanes(f)], first_s.at[6 + k], first_r.at[6 + k], (r, peer)))
    locals_ = [
        pltpu.make_async_copy(small_ref, small_buf.at[f], first_l.at[0]),
        pltpu.make_async_copy(feat_ref.at[own_rows], x_buf.at[:, lanes(f)], first_l.at[1]),
        pltpu.make_async_copy(whead_ref, whead.at[lanes(f)], first_l.at[2]),
    ]

    def y_copy(s, m):
        u, span = 3 * s + m, rows_of(q, 0, quarter)
        return remote(weights[m].at[s, span], wfull.at[s, m, f, span], fy_s.at[u], fy_r.at[u], (r, far))

    def a_copy(s, m):
        u, span = 3 * s + m, rows_of(q_d, 0, cut_b)
        return remote(weights[m].at[s, span], wfull.at[s, m, f, span], a_s.at[u], a_r.at[u], (r, far))

    def own_copy(s, m):
        u = 3 * s + m
        return remote(weights[m].at[s], wfull.at[s, m, f], own_s.at[u], own_r.at[u], (r, core))

    def pass_on(s, m, span, send, recv, device):
        u, ref = 3 * s + m, wfull.at[s, m, far, span]
        return remote(ref, ref, send.at[u], recv.at[u], device)

    def x_copy(s, m):
        return pass_on(s, m, rows_of(q, 0, quarter), x_s, x_r, (rx, f))

    def z_copy(s, m):
        return pass_on(s, m, rows_of(q, 0, quarter), z_s, z_r, (rz, f))

    def b_copy(s, m):
        return pass_on(s, m, rows_of(q_z, cut_b, cut_c - cut_b), b_s, b_r, (rx, f))

    def c_copy(s, m):
        return pass_on(s, m, rows_of(q_x, cut_c, quarter - cut_c), c_s, c_r, (rz, f))

    def far_copy(s, m):
        u, ref = 3 * s + m, wfull.at[s, m, far]
        return remote(ref, ref, far_s.at[u], far_r.at[u], (r, core))

    def w_load(s, m):
        copies = [pltpu.make_async_copy(weights[m].at[s], weight.at[m, :, lanes(f)], load_w.at[m, 0])]
        for k, b in enumerate(others):
            copies.append(
                pltpu.make_async_copy(wfull.at[s, m, b], weight.at[m, :, lanes(b)], load_w.at[m, 1 + k])
            )
        return copies

    def start(copies):
        for copy in copies:
            copy.start()

    def wait(copies):
        for copy in copies:
            copy.wait()

    def send_own(s):
        for m in range(3):
            y_copy(s, m).start()
            a_copy(s, m).start()
            own_copy(s, m).start()

    send_own(0)
    start(firsts + locals_)

    @pl.loop(1, sections)
    def _(s):
        send_own(s)

    start(heads)

    def arrange():
        for copy in firsts:
            copy.wait_recv()
        wait(locals_)
        par[...] = jnp.concatenate([small_buf[b] for b in range(blocks)], axis=1)
        logits = par[0:8]
        probs = jnp.exp(logits - jnp.max(logits, axis=1, keepdims=True))
        probs = probs / jnp.sum(probs, axis=1, keepdims=True)
        par[0:sections] = (width * probs)[0:sections]
        hs[0] = x_buf[...]

    def put(value, at_rows):
        for k, piece in enumerate(split(value)):
            upper[k, :, at_rows] = piece

    low_cols, high_cols = slice(0, width), slice(width, 2 * width)

    def product(s, m):
        tiles = []
        for t in range(2):
            w = split(weight[m, :, t * half : (t + 1) * half])
            tiles.append(dot3((upper[0], upper[1]), w, NN))
        return jnp.concatenate(tiles, axis=1) + par[pl.ds(sections * (m + 1) + s, 1), :]

    def gate(s, m):
        if m == 0:
            put(hs[s], low_cols)
            put(x_buf[...] * par[pl.ds(s, 1), :], high_cols)
            zs[s] = jax.nn.sigmoid(product(s, 0))
        elif m == 1:
            rs[s] = jax.nn.sigmoid(product(s, 1))
            put(rs[s] * hs[s], low_cols)
        else:
            cand = jnp.tanh(product(s, 2))
            cs[s] = cand
            hs[s + 1] = hs[s] + zs[s] * (cand - hs[s])

    def at(step, m, back_by):
        u = m - back_by
        return step + u // 3, u % 3

    @pl.loop(0, sections + 1)
    def _(step):
        for m in range(3):

            @pl.when(step < sections)
            def _():
                y_copy(step, m).wait_recv()
                x_copy(step, m).start()
                z_copy(step, m).start()

            s1, m1 = at(step, m, 1)

            @pl.when((s1 >= 0) & (s1 < sections))
            def _():
                x_copy(s1, m1).wait_recv()
                z_copy(s1, m1).wait_recv()
                b_copy(s1, m1).start()
                c_copy(s1, m1).start()

            s2, m2 = at(step, m, 2)

            @pl.when((s2 >= 0) & (s2 < sections))
            def _():
                a_copy(s2, m2).wait_recv()
                b_copy(s2, m2).wait_recv()
                c_copy(s2, m2).wait_recv()
                far_copy(s2, m2).start()

            if m == 0:
                pl.when(step == 1)(arrange)

            @pl.when(step >= 1)
            def _():
                own_copy(step - 1, m).wait_recv()
                far_copy(step - 1, m).wait_recv()
                copies = w_load(step - 1, m)
                start(copies)
                wait(copies)
                gate(step - 1, m)

    def feat_step(n, src, slots):
        return [
            remote(src, slots.at[f], ef_s.at[n, k], ef_r.at[n, k], (r, peer)) for k, peer in enumerate(others)
        ]

    def rows_step(n, src, slots):
        return [
            remote(src, slots.at[r], er_s.at[n, k - 1], er_r.at[n, k - 1], (lax.rem(r + k, rows), f))
            for k in range(1, rows)
        ]

    def sum_all(n, value, src, feat_slots, row_slots, merge):
        feat_slots[f] = value
        src[...] = value
        copies = feat_step(n, src, feat_slots)
        start(copies)
        wait(copies)
        value = merge(feat_slots)
        row_slots[r] = value
        src[...] = value
        copies = rows_step(n, src, row_slots)
        start(copies)
        return copies

    for m in (2, 0, 1):
        start(w_load(sections - 1, m))
    here = pl.ds(pl.multiple_of(f * mine, mine), mine)
    place = lax.broadcasted_iota(jnp.int32, (1, mine), 1) + f * mine
    flat = jnp.where(place < count_ref[0], 1.0, 0.0) * valid_ref[:, here].astype(F32)
    column = jnp.transpose(jnp.broadcast_to(flat, (8, mine)))[:, 0:1]
    wout_buf[...] = jnp.zeros_like(wout_buf)
    wout_buf[0:classes] = wout_ref[...]
    dlog_buf[...] = jnp.zeros_like(dlog_buf)
    dlog_buf[0:classes] = cot_ref[:, here] * flat
    turn[...] = jnp.zeros_like(turn)
    turn[0:1, 0:classes] = bout_ref[...]
    b_out = jnp.transpose(turn[...])[0:TALL, 0:1]
    current = hs[sections]
    count = jnp.sum(column, axis=0, keepdims=True)
    sums = jnp.sum(column * current, axis=0, keepdims=True)
    gap = current - sums / jnp.maximum(count, 1.0)
    square = jnp.sum(column * gap * gap, axis=0, keepdims=True)
    stats = jnp.concatenate(
        [jnp.broadcast_to(count, sums.shape), sums, square, jnp.zeros((5, width), F32)], axis=0
    )
    wait(sum_all(0, stats, ex_a, ex_a_feat, ex_a_rows, merge_stats))
    stats = merge_stats(ex_a_rows)
    count = stats[0:1]
    inv_std = lax.rsqrt(stats[2:3] / count + 1e-05)
    x_hat[...] = (current - stats[1:2] / count) * inv_std
    gain, shift = par[4 * sections : 4 * sections + 1], par[4 * sections + 1 : 4 * sections + 2]
    normed = split(x_hat[...] * gain + shift)
    for copy in heads:
        copy.wait_recv()
    w_head = split(whead[...])
    act = dot3(normed, w_head, NN) + bhead_ref[...]
    phi = 0.5 * (1.0 + lax.erf(act * 0.7071067811865476))
    hidden = split(act * phi)
    slope = phi + act * (jnp.exp(-0.5 * act * act) * 0.3989422804014327)
    w_out = split(wout_buf[...])
    logit_buf[f] = (dot3(w_out, hidden, NT) + b_out) * flat
    logit_copies = [
        remote(logit_buf.at[f], logit_buf.at[f], logit_s.at[k], logit_r.at[k], (r, peer))
        for k, peer in enumerate(others)
    ]
    start(logit_copies)
    d_log = dlog_buf[...]
    d_act = dot3(split(d_log), w_out, TN) * slope
    d_act2 = split(d_act)
    d_normed = dot3(d_act2, w_head, NT)
    sums = jnp.concatenate(
        [
            jnp.sum(d_normed * x_hat[...], axis=0, keepdims=True),
            jnp.sum(d_normed, axis=0, keepdims=True),
            jnp.zeros((6, width), F32),
        ],
        axis=0,
    )
    dh[...] = d_normed
    copies = sum_all(1, sums, ex_b, ex_b_feat, ex_b_rows, sum_slots)
    vec[...] = jnp.zeros_like(vec)
    hid = act.shape[1]
    aux = 4 * sections
    vec[aux : aux + TALL, 0:hid] = dot3(split(d_log), hidden, NN)
    vec[aux + classes : aux + classes + 1, 0:hid] = jnp.sum(d_act, axis=0, keepdims=True)
    ones = jnp.ones((8, mine), F32)
    vec[aux + classes + 1 : aux + classes + 2, 0:TALL] = dot3(split(ones), split(d_log), NT)[0:1]
    grad = dot3(normed, d_act2, TN)
    for b in range(blocks):
        for t in range(hid // LANES):
            h_grads[b, t * LANES : (t + 1) * LANES] = grad[
                b * LANES : (b + 1) * LANES, t * LANES : (t + 1) * LANES
            ]
    wait(copies)
    sums = sum_slots(ex_b_rows)
    dh[...] = inv_std * (
        dh[...] * gain - column / count * gain * (sums[1:2] + x_hat[...] * sums[0:1])
    )
    tiny_out[...] = sums
    gin[...] = jnp.zeros_like(gin)

    outs = (go_out, gz_out, gr_out)
    which = (2, 0, 1)
    peers = [(flip(r, 2**k), f) for k in range(levels)]
    piece = depth // CUTS
    held, landed = rings(levels)

    class Unit:
        def __init__(self, step, j):
            m, cut = j // CUTS, j % CUTS
            span = pl.ds(cut * piece, piece)
            where = (step % 3) * SLOTS + j
            self.depth = piece
            self.grads = grads.at[(3 * step + m) % 2, :, span]
            self.core, self.total, self.land = core_buf.at[j], total.at[step % held, j], land.at[step % landed, j]
            self.out = outs[m].at[sections - 1 - step, span]
            self.core_sems = [(core_s.at[k, j], core_r.at[k, j]) for k in range(2)]
            self.rs_sems = [(rs_s.at[k, step % landed, j], rs_r.at[k, step % landed, j]) for k in range(levels + 2)]
            self.ag_sems = [(ag_s.at[k, where], ag_r.at[k, where]) for k in range(levels)]
            self.out_sem = out_l.at[where]
            self.plan(["y"] + list(range(levels)) if j < SLOTS - 1 else [1, "y", 0] + list(range(2, levels)))

        def plan(self, order):
            self.moves, self.backs = [], []
            base, size, block_list, landing, sem = 0, self.depth, [0, 1], 0, 0
            for step in order:
                move = []
                if step == "y":
                    device, sent, kept, from_blocks, block_list = (r, far), base, base, [1], [0]
                else:
                    size //= 2
                    side = (r // 2**step) % 2
                    device, sent, kept, from_blocks = (
                        peers[step], base + (1 - side) * size, base + side * size, block_list,
                    )
                    self.backs.append((device, part(kept, size)))
                for k, block in enumerate(from_blocks):
                    move.append(
                        (device, block, part(sent, size), block_list[k], part(kept, size),
                         pl.ds(landing, size), self.rs_sems[sem])
                    )
                    landing += size
                    sem += 1
                self.moves.append(move)
                base = kept
            self.backs.reverse()

        def core_copies(self):
            return [
                remote(self.grads.at[b], self.core.at[k], *self.core_sems[k], (r, core))
                for k, b in enumerate((core, both))
            ]

        def rs_copies(self, i):
            return [
                remote(self.total.at[block, sent], self.land.at[landing], *sems, device)
                for device, block, sent, _, _, landing, sems in self.moves[i]
            ]

        def add(self, i):
            for _, _, _, block, kept, landing, _ in self.moves[i]:
                self.total[block, kept] += self.land[landing]

        def ag_copy(self, i):
            device, kept = self.backs[i]
            dst = self.out.at[kept]
            return remote(self.total.at[0, kept] if i == 0 else dst, dst, *self.ag_sems[i], device)

        def out_local(self):
            kept = self.backs[0][1]
            return pltpu.make_async_copy(self.total.at[0, kept], self.out.at[kept], self.out_sem)

    class HeadUnit(Unit):
        def __init__(self):
            self.depth = h_grads.shape[1]
            self.grads, self.core, self.total, self.land, self.out = h_grads, h_core, h_total, h_land, ghead_out
            sems = [(hu_s.at[k], hu_r.at[k]) for k in range(2 * levels + 4)]
            self.core_sems, self.rs_sems, self.ag_sems = sems[:2], sems[2 : levels + 4], sems[levels + 4 :]
            self.out_sem = hu_l.at[0]
            self.plan(["y"] + list(range(levels)))

    def stage_core(unit):
        wait(unit.core_copies())
        unit.total[1] = unit.grads[far] + unit.core[1]
        unit.total[0] = unit.grads[f] + unit.core[0]
        start(unit.rs_copies(0))

    def stage_sum(i, unit):
        wait(unit.rs_copies(i))
        unit.add(i)
        if i < levels:
            start(unit.rs_copies(i + 1))
        else:
            unit.ag_copy(0).start()
            unit.out_local().start()

    def stage_out(i, unit):
        if i == 0:
            unit.out_local().wait()
        unit.ag_copy(i).wait()
        if i + 1 < levels:
            unit.ag_copy(i + 1).start()

    stages = [stage_core]
    stages += [functools.partial(stage_sum, i) for i in range(levels + 1)]
    stages += [functools.partial(stage_out, i) for i in range(levels)]

    def outer(m, u, right):
        for t in range(2):
            tile = split(right[:, t * half : (t + 1) * half])
            tile = dot3((upper[0], upper[1]), tile, TN)
            for b in range(half // LANES):
                grads[u % 2, t * (half // LANES) + b] = tile[:, b * LANES : (b + 1) * LANES]

    def back(m, left, t):
        return dot3(left, split(weight[which[m], t * half : (t + 1) * half, :]), NT)

    def compute(step, m):
        s = sections - 1 - step
        u = 3 * step + m
        wait(w_load(s, which[m]))
        h = hs[s]
        if m == 0:
            z, reset, c = zs[s], rs[s], cs[s]
            put(reset * h, low_cols)
            put(x_buf[...] * par[pl.ds(s, 1), :], high_cols)
            d_out = dh[...] * z * (1.0 - c * c)
            vec[pl.ds(2 * sections + s, 1), :] = jnp.sum(d_out, axis=0, keepdims=True)
            outer(m, u, d_out)
            left = split(d_out)
            for t in range(4):
                d_in[:, t * half : (t + 1) * half] = back(m, left, t)
            d_reset[...] = d_in[:, 0:width] * h * reset * (1.0 - reset)
        elif m == 1:
            z, reset, c = zs[s], rs[s], cs[s]
            put(h, low_cols)
            d_up = dh[...] * (c - h) * z * (1.0 - z)
            vec[pl.ds(s, 1), :] = jnp.sum(d_up, axis=0, keepdims=True)
            outer(m, u, d_up)
            dh[...] = dh[...] * (1.0 - z) + d_in[:, 0:width] * reset
            left = split(d_up)
            for t in range(4):
                cols = slice(t % 2 * half, (t % 2 + 1) * half)
                if t < 2:
                    dh[:, cols] += back(m, left, t)
                else:
                    d_in[:, t * half : (t + 1) * half] += back(m, left, t)
        else:
            d_r = d_reset[...]
            vec[pl.ds(sections + s, 1), :] = jnp.sum(d_r, axis=0, keepdims=True)
            outer(m, u, d_r)
            left = split(d_r)
            for t in range(4):
                cols = slice(t % 2 * half, (t % 2 + 1) * half)
                if t < 2:
                    dh[:, cols] += back(m, left, t)
                else:
                    d_xs = d_in[:, t * half : (t + 1) * half] + back(m, left, t)
                    gin[:, cols] += d_xs * par[pl.ds(s, 1), cols]
                    vec[pl.ds(3 * sections + s, 1), cols] = jnp.sum(d_xs * x_buf[:, cols], axis=0, keepdims=True)

        @pl.when(step + 1 < sections)
        def _():
            start(w_load(s - 1, which[m]))

    gf_copies = [
        remote(gin.at[:, lanes(peer)], gfeat_out.at[own_rows], gf_s.at[k], gf_r.at[k], (r, peer))
        for k, peer in enumerate(others)
    ]
    gf_local = pltpu.make_async_copy(gin.at[:, lanes(f)], gfeat_out.at[own_rows], gf_l.at[0])
    vec_feat = feat_step(2, vec, ex_c_feat)
    vec_rows = rows_step(2, vec, ex_c_rows)

    start(HeadUnit().core_copies())

    def before(step, j, back_by):
        u = j - back_by
        return step + u // SLOTS, u % SLOTS

    delays = schedule(levels)

    @pl.loop(0, sections + -(-delays[-1] // SLOTS))
    def _(step):
        for j in range(SLOTS):

            @pl.when(step < sections)
            def _():
                if j % CUTS == 0:
                    compute(step, j // CUTS)
                start(Unit(step, j).core_copies())

            for delay, stage in zip(delays, stages, strict=True):
                s1, j1 = before(step, j, delay)
                if j1 == SLOTS - 1:

                    @pl.when(s1 == -1)
                    def _():
                        stage(HeadUnit())

                @pl.when((s1 >= 0) & (s1 < sections))
                def _():
                    stage(Unit(s1, j1))

            if j == 0:

                @pl.when(step == sections)
                def _():
                    ex_c_feat[f] = vec[...]
                    start(vec_feat)
                    gin[...] += dh[...]
                    start(gf_copies + [gf_local])

            if j == 2:

                @pl.when(step == sections)
                def _():
                    wait(vec_feat)
                    vec[...] = sum_slots(ex_c_feat)
                    ex_c_rows[r] = vec[...]
                    start(vec_rows)

    wait(vec_rows)
    sums = sum_slots(ex_c_rows)
    scale, gsc = par[0:sections], sums[3 * sections : 4 * sections]
    vec_out[...] = sums
    vec_out[3 * sections : 4 * sections] = scale * (gsc - jnp.sum(scale * gsc, axis=1, keepdims=True) / width)
    wait(gf_copies + [gf_local])
    wait(logit_copies)
    for b in range(blocks):
        logit_out[:, b * mine : (b + 1) * mine] = logit_buf[b]

    @pl.loop(0, sections)
    def _(s):
        for m in range(3):
            for copy in (y_copy, a_copy, own_copy, x_copy, z_copy, b_copy, c_copy, far_copy):
                copy(s, m).wait_send()

    for copy in firsts + heads:
        copy.wait_send()


def finish_kernel(
    sections, classes,
    gz_ref, gr_ref, go_ref, gfeat_ref, ghead_ref, logit_ref, tiny_ref, vec_ref,
    logit_out, gfeat_out, gmask_out, gz_out, gr_out, go_out, bz_out, br_out, bo_out,
    gain_out, shift_out, ghead_out, bhead_out, wout_out, bout_out,
    big, feat, head, load, store,
):
    f = lax.axis_index("feat")
    pairs = [(feat, gfeat_ref, gfeat_out)] + [
        (big.at[m, s], src.at[s], dst.at[s])
        for s in range(sections)
        for m, (src, dst) in enumerate(((gz_ref, gz_out), (gr_ref, gr_out), (go_ref, go_out)))
    ]
    loads = [pltpu.make_async_copy(src, held, load.at[k]) for k, (held, src, _) in enumerate(pairs)]
    stores = [pltpu.make_async_copy(held, dst, store.at[k]) for k, (held, _, dst) in enumerate(pairs)]
    for copy in loads:
        copy.start()
    block = feat.shape[1]
    cols = pl.ds(pl.multiple_of(f * block, block), block)
    hidden = bhead_out.shape[1]
    aux = 4 * sections
    logit_out[...] = logit_ref[0:classes]
    for k, out in enumerate((bz_out, br_out, bo_out, gmask_out)):
        out[...] = vec_ref[k * sections : (k + 1) * sections, cols]
    gain_out[...] = tiny_ref[0:1, cols]
    shift_out[...] = tiny_ref[1:2, cols]
    for t in range(hidden // block):
        ghead_out[:, t * block : (t + 1) * block] = ghead_ref[t * block : (t + 1) * block]
    wout_out[...] = vec_ref[aux : aux + classes, 0:hidden]
    bhead_out[...] = vec_ref[aux + classes : aux + classes + 1, 0:hidden]
    bout_out[...] = vec_ref[aux + classes + 1 : aux + classes + 2, 0:classes]
    for load_, store_ in zip(loads, stores, strict=True):
        load_.wait()
        store_.start()
    for copy in stores:
        copy.wait()


def layer(
    rows, groups, features, w_update, w_reset, w_candidate, w_head, counts, validity, mask_logits, b_update, b_reset,
    b_candidate, norm_gain, norm_shift, b_head, w_out, b_out, cotangent,
):
    sections, depth, block = w_update.shape
    width, mine = groups * block, features.shape[0] // groups
    hidden = w_head.shape[1]
    classes = w_out.shape[0]
    units = 3 * sections
    levels = rows.bit_length() - 1
    head_depth = max(hidden, 8 * rows)
    piece = depth // CUTS
    held, landed = rings(levels)
    long = 4 * sections + TALL
    sds = jax.ShapeDtypeStruct
    dma = pltpu.SemaphoreType.DMA
    any_, vmem = pl.BlockSpec(memory_space=pl.ANY), pl.BlockSpec(memory_space=pltpu.VMEM)
    grad = sds((sections, depth, block), F32)

    def buf(*shape):
        return pltpu.VMEM(shape, F32)

    made = pl.pallas_call(
        functools.partial(kernel, sections, rows, levels, classes),
        out_shape=[
            grad, grad, grad,
            sds(features.shape, F32),
            sds((head_depth, block), F32),
            sds((TALL, groups * mine), F32),
            sds((8, width), F32),
            sds((long, width), F32),
            sds((sections, 3, groups, depth, block), F32),
        ],
        in_specs=[any_] * 5 + [pl.BlockSpec(memory_space=pltpu.SMEM)] + [vmem] * 11,
        out_specs=[any_] * 5 + [vmem] * 3 + [any_],
        scratch_shapes=[
            buf(mine, width), buf(groups, PAR, block), buf(PAR, width), buf(sections + 1, mine, width),
            buf(sections, mine, width), buf(sections, mine, width), buf(sections, mine, width),
            buf(3, depth, width), pltpu.VMEM((2, mine, depth), BF16),
            buf(width, hidden), buf(mine, width), buf(groups, TALL, mine), buf(mine, width),
            buf(mine, depth), buf(mine, width), buf(mine, width), buf(long, width),
            buf(PAR, block), buf(TALL, hidden), buf(TALL, mine), buf(8, LANES),
            buf(2, groups, depth, block), buf(SLOTS, 2, piece, block), buf(held, SLOTS, 2, piece, block),
            buf(landed, SLOTS, 2 * piece, block),
            buf(groups, head_depth, block), buf(2, head_depth, block), buf(2, head_depth, block),
            buf(2 * head_depth, block),
            buf(8, width), buf(groups, 8, width), buf(rows, 8, width),
            buf(8, width), buf(groups, 8, width), buf(rows, 8, width),
            buf(groups, long, width), buf(rows, long, width),
            dma((9,)), dma((9,)), dma((3,)),
        ] + [dma((units,))] * 16 + [
            dma((3, groups)), dma((3,)), dma((3,)), dma((3,)), dma((3,)), dma((1,)),
            dma((3, 3)), dma((3, 3)), dma((3, rows - 1)), dma((3, rows - 1)),
            dma((2, SLOTS)), dma((2, SLOTS)), dma((levels + 2, landed, SLOTS)), dma((levels + 2, landed, SLOTS)),
            dma((levels, 3 * SLOTS)), dma((levels, 3 * SLOTS)), dma((3 * SLOTS,)),
            dma((2 * levels + 4,)), dma((2 * levels + 4,)), dma((1,)),
        ],
        compiler_params=pltpu.CompilerParams(
            collective_id=0, has_side_effects=True, vmem_limit_bytes=62 * 2**20
        ),
    )(
        features, w_update, w_reset, w_candidate, w_head, counts, validity[None], mask_logits, b_update, b_reset,
        b_candidate, norm_gain[None], norm_shift[None], b_head[None], w_out, b_out[None], cotangent,
    )
    row = sds((1, block), F32)
    bias = sds((sections, block), F32)
    return pl.pallas_call(
        functools.partial(finish_kernel, sections, classes),
        out_shape=[
            sds((classes, groups * mine), F32), sds(features.shape, F32), bias, grad, grad, grad, bias, bias, bias,
            row, row, sds((block, hidden), F32), sds((1, hidden), F32), sds((classes, hidden), F32),
            sds((1, classes), F32),
        ],
        in_specs=[any_] * 4 + [vmem] * 4,
        out_specs=[vmem, any_, vmem, any_, any_, any_] + [vmem] * 9,
        scratch_shapes=[
            buf(3, sections, depth, block), buf(*features.shape), buf(8, LANES),
            dma((units + 1,)), dma((units + 1,)),
        ],
        compiler_params=pltpu.CompilerParams(vmem_limit_bytes=62 * 2**20),
    )(*made[:8])


def local(
    rows, groups, features, counts, validity, mask_logits, w_update, w_reset, w_candidate, b_update, b_reset,
    b_candidate, norm_gain, norm_shift, w_head, b_head, w_out, b_out, cotangent,
):
    out = layer(
        rows, groups, features, w_update, w_reset, w_candidate, w_head, counts, validity, mask_logits, b_update,
        b_reset, b_candidate, norm_gain, norm_shift, b_head, w_out.T, b_out, cotangent.T,
    )
    logits, g_feat, g_mask, gz, gr, go, bz, br, bo, gain, shift, g_head, g_b_head, g_w_out, g_b_out = out
    return (
        logits.T, g_feat, g_mask, gz, gr, go, bz, br, bo, gain[0], shift[0], g_head, g_b_head[0], g_w_out.T,
        g_b_out[0],
    )


def solution(mesh):
    rows, groups = mesh.shape["rows"], mesh.shape["feat"]
    split_cols, by_feat = P(None, None, "feat"), P("feat")
    return jax.shard_map(
        functools.partial(local, rows, groups),
        mesh=mesh,
        in_specs=(
            P("rows", "feat"), P("rows"), P("rows"), P(None, "feat"), split_cols, split_cols, split_cols,
            P(None, "feat"), P(None, "feat"), P(None, "feat"), by_feat, by_feat, P("feat", None),
            P(), P(), P(), P("rows", None),
        ),
        out_specs=(
            P("rows", None), P("rows", "feat"), P(None, "feat"), split_cols, split_cols, split_cols,
            P(None, "feat"), P(None, "feat"), P(None, "feat"), by_feat, by_feat, P("feat", None),
            P(), P(), P(),
        ),
        check_vma=False,
    )
```

```python
import functools

import jax
import jax.numpy as jnp
from jax import lax
from jax.experimental import pallas as pl
from jax.experimental.pallas import tpu as pltpu
from jax.sharding import PartitionSpec as P

MESH = pl.DeviceIdType.MESH
F32, BF16 = jnp.float32, jnp.bfloat16
LANES = 128
PAR = 32
TALL = 16


def cuts_of(levels):
    return 4 if levels < 6 else 2


def early(levels):
    return ((0, 3, 4, 7, 10), (2, 8), (3, 8)) if levels < 6 else ((5,),) * 3


def schedule(levels):
    if levels == 3:
        return [1, 4, 7, 9, 11, 13, 15, 18]
    sums = [1, 4, 7, 9] + [9 + k for k in range(1, levels - 1)]
    gap = 2 if levels < 4 else 1
    return sums + [sums[-1] + 1 + gap * k for k in range(levels)]


def rings(levels):
    return -(-(schedule(levels)[levels + 2] + 1) // (3 * cuts_of(levels))), 2


def flip(index, stride):
    return index + stride - 2 * stride * ((index // stride) % 2)


def split(value):
    high = value.astype(BF16)
    return high, (value - high.astype(F32)).astype(BF16)


def dot3(left, right, dims):
    def one(a, b):
        return lax.dot_general(a, b, (dims, ((), ())), preferred_element_type=F32)

    return one(left[0], right[1]) + one(left[1], right[0]) + one(left[0], right[0])


NN, NT, TN = ((1,), (0,)), ((1,), (1,)), ((0,), (0,))


def remote(src, dst, send, recv, device):
    return pltpu.make_async_remote_copy(
        src_ref=src, dst_ref=dst, send_sem=send, recv_sem=recv, device_id=device, device_id_type=MESH
    )


def meet(devices):
    barrier = pltpu.get_barrier_semaphore()
    for device in devices:
        pl.semaphore_signal(barrier, inc=1, device_id=device, device_id_type=MESH)
    pl.semaphore_wait(barrier, len(devices))


def sum_slots(ref):
    total = ref[0]
    for k in range(1, ref.shape[0]):
        total = total + ref[k]
    return total


def merge_stats(blocks, ref):
    parts = [ref[k] for k in range(ref.shape[0])]
    counts = [p[2 * blocks : 2 * blocks + 1] for p in parts]
    count = functools.reduce(jnp.add, counts)
    sums = functools.reduce(jnp.add, [p[0:blocks] for p in parts])
    mean = sums / jnp.maximum(count, 1.0)
    square = jnp.zeros_like(sums)
    for p, n in zip(parts, counts, strict=True):
        gap = p[0:blocks] / jnp.maximum(n, 1.0) - mean
        square = square + (p[blocks : 2 * blocks] + n * gap * gap)
    rest = ref.shape[1] - 2 * blocks - 1
    return jnp.concatenate([sums, square, count, jnp.zeros((rest, LANES), F32)], axis=0)


def stack(row):
    return [row[:, k * LANES : (k + 1) * LANES] for k in range(row.shape[1] // LANES)]


def unstack(value):
    return jnp.concatenate([value[k : k + 1] for k in range(value.shape[0])], axis=1)


def kernel(
    sections, rows, levels, classes,
    feat_ref, wz_ref, wr_ref, wo_ref, whead_ref, count_ref, valid_ref,
    mask_ref, bz_ref, br_ref, bo_ref, gain_ref, shift_ref, bhead_ref, wout_ref, bout_ref, cot_ref,
    gz_out, gr_out, go_out, gfeat_out, ghead_out, logit_out, tiny_out, own_out, aux_out, wfull,
    x_buf, small_buf, par, hs, zs, rs, cs, weight, upper,
    whead, x_hat, logit_buf, dh, d_in, d_reset, gin, vec,
    small_ref, wout_buf, dlog_buf, turn,
    grads, core_buf, total, land,
    h_grads, h_core, h_total, h_land,
    ex_a, ex_a_feat, ex_a_rows, ex_b, ex_b_feat, ex_b_rows,
    ex_c, ex_c_feat, ex_c_mid, ex_c_rows, ex_d, ex_d_feat,
    first_s, first_r, first_l, fy_s, fy_r, a_s, a_r, x_s, x_r, z_s, z_r, b_s, b_r, c_s, c_r,
    own_s, own_r, far_s, far_r, load_w, logit_s, logit_r, gf_s, gf_r, gf_l,
    ef_s, ef_r, er_s, er_r,
    core_s, core_r, rs_s, rs_r, ag_s, ag_r, out_l, hu_s, hu_r, hu_l,
):
    r, f = lax.axis_index("rows"), lax.axis_index("feat")
    weights = (wz_ref, wr_ref, wo_ref)
    units = 3 * sections
    depth = wz_ref.shape[1]
    cuts = cuts_of(levels)
    slots = 3 * cuts
    mine, width = x_buf.shape
    blocks = small_buf.shape[0]
    half = width // 2
    core, far, both = flip(f, 1), flip(f, 2), flip(flip(f, 1), 2)
    others = (core, far, both)
    rx, rz = flip(r, 1), flip(r, 2)
    quarter = depth // 4
    cut_b, cut_c = 3 * quarter // 8, 3 * quarter // 8 + 5 * quarter // 16
    q = 2 * (r % 2) + (r // 2) % 2
    q_x, q_z, q_d = flip(q, 2), flip(q, 1), flip(flip(q, 1), 2)

    def lanes(index):
        return pl.ds(pl.multiple_of(index * LANES, LANES), LANES)

    def part(start, size):
        return pl.ds(pl.multiple_of(start, 8), size)

    def rows_of(index, start, size):
        return part(index * quarter + start, size)

    meet([(r, peer) for peer in others] + [(lax.rem(r + k, rows), f) for k in range(1, rows)])

    small_ref[...] = jnp.zeros_like(small_ref)
    for k, ref in enumerate((mask_ref, bz_ref, br_ref, bo_ref)):
        small_ref[k * sections : (k + 1) * sections] = ref[...]
    small_ref[4 * sections : 4 * sections + 1] = gain_ref[...]
    small_ref[4 * sections + 1 : 4 * sections + 2] = shift_ref[...]
    own_rows = pl.ds(pl.multiple_of(f * mine, mine), mine)
    firsts, heads = [], []
    for k, peer in enumerate(others):
        chunk = pl.ds(pl.multiple_of(peer * mine, mine), mine)
        firsts += [
            remote(small_ref, small_buf.at[f], first_s.at[k], first_r.at[k], (r, peer)),
            remote(feat_ref.at[chunk], x_buf.at[:, lanes(f)], first_s.at[3 + k], first_r.at[3 + k], (r, peer)),
        ]
        heads.append(remote(whead_ref, whead.at[lanes(f)], first_s.at[6 + k], first_r.at[6 + k], (r, peer)))
    locals_ = [
        pltpu.make_async_copy(small_ref, small_buf.at[f], first_l.at[0]),
        pltpu.make_async_copy(feat_ref.at[own_rows], x_buf.at[:, lanes(f)], first_l.at[1]),
        pltpu.make_async_copy(whead_ref, whead.at[lanes(f)], first_l.at[2]),
    ]

    def y_copy(s, m):
        u, span = 3 * s + m, rows_of(q, 0, quarter)
        return remote(weights[m].at[s, span], wfull.at[s, m, f, span], fy_s.at[u], fy_r.at[u], (r, far))

    def a_copy(s, m):
        u, span = 3 * s + m, rows_of(q_d, 0, cut_b)
        return remote(weights[m].at[s, span], wfull.at[s, m, f, span], a_s.at[u], a_r.at[u], (r, far))

    def own_copy(s, m):
        u = 3 * s + m
        return remote(weights[m].at[s], wfull.at[s, m, f], own_s.at[u], own_r.at[u], (r, core))

    def pass_on(s, m, span, send, recv, device):
        u, ref = 3 * s + m, wfull.at[s, m, far, span]
        return remote(ref, ref, send.at[u], recv.at[u], device)

    def x_copy(s, m):
        return pass_on(s, m, rows_of(q, 0, quarter), x_s, x_r, (rx, f))

    def z_copy(s, m):
        return pass_on(s, m, rows_of(q, 0, quarter), z_s, z_r, (rz, f))

    def b_copy(s, m):
        return pass_on(s, m, rows_of(q_z, cut_b, cut_c - cut_b), b_s, b_r, (rx, f))

    def c_copy(s, m):
        return pass_on(s, m, rows_of(q_x, cut_c, quarter - cut_c), c_s, c_r, (rz, f))

    def far_copy(s, m):
        u, ref = 3 * s + m, wfull.at[s, m, far]
        return remote(ref, ref, far_s.at[u], far_r.at[u], (r, core))

    def w_load(s, m):
        copies = [pltpu.make_async_copy(weights[m].at[s], weight.at[m, :, lanes(f)], load_w.at[m, 0])]
        for k, b in enumerate(others):
            copies.append(
                pltpu.make_async_copy(wfull.at[s, m, b], weight.at[m, :, lanes(b)], load_w.at[m, 1 + k])
            )
        return copies

    def start(copies):
        for copy in copies:
            copy.start()

    def wait(copies):
        for copy in copies:
            copy.wait()

    def send_own(s):
        for m in range(3):
            y_copy(s, m).start()
            a_copy(s, m).start()
            own_copy(s, m).start()

    send_own(0)
    start(firsts + locals_)

    @pl.loop(1, sections)
    def _(s):
        send_own(s)

    start(heads)

    def arrange():
        for copy in firsts:
            copy.wait_recv()
        wait(locals_)
        par[...] = jnp.concatenate([small_buf[b] for b in range(blocks)], axis=1)
        logits = par[0:8]
        probs = jnp.exp(logits - jnp.max(logits, axis=1, keepdims=True))
        probs = probs / jnp.sum(probs, axis=1, keepdims=True)
        par[0:sections] = (width * probs)[0:sections]
        hs[0] = x_buf[...]

    def put(value, at_rows):
        for k, piece in enumerate(split(value)):
            upper[k, :, at_rows] = piece

    low_cols, high_cols = slice(0, width), slice(width, 2 * width)

    def product(s, m):
        tiles = []
        for t in range(2):
            w = split(weight[m, :, t * half : (t + 1) * half])
            tiles.append(dot3((upper[0], upper[1]), w, NN))
        return jnp.concatenate(tiles, axis=1) + par[pl.ds(sections * (m + 1) + s, 1), :]

    def gate(s, m):
        if m == 0:
            put(hs[s], low_cols)
            put(x_buf[...] * par[pl.ds(s, 1), :], high_cols)
            zs[s] = jax.nn.sigmoid(product(s, 0))
        elif m == 1:
            rs[s] = jax.nn.sigmoid(product(s, 1))
            put(rs[s] * hs[s], low_cols)
        else:
            cand = jnp.tanh(product(s, 2))
            cs[s] = cand
            hs[s + 1] = hs[s] + zs[s] * (cand - hs[s])

    def at(step, m, back_by):
        u = m - back_by
        return step + u // 3, u % 3

    @pl.loop(0, sections + 2)
    def _(step):
        for m in range(3):

            @pl.when(step < sections)
            def _():
                y_copy(step, m).wait_recv()
                x_copy(step, m).start()
                z_copy(step, m).start()

            s1, m1 = at(step, m, 1)

            @pl.when((s1 >= 0) & (s1 < sections))
            def _():
                x_copy(s1, m1).wait_recv()
                z_copy(s1, m1).wait_recv()
                b_copy(s1, m1).start()
                c_copy(s1, m1).start()

            s2, m2 = at(step, m, 2)

            @pl.when((s2 >= 0) & (s2 < sections))
            def _():
                a_copy(s2, m2).wait_recv()
                b_copy(s2, m2).wait_recv()
                c_copy(s2, m2).wait_recv()
                far_copy(s2, m2).start()

            s3, m3 = at(step, m, 3)

            @pl.when((s3 >= 0) & (s3 < sections))
            def _():
                own_copy(s3, m3).wait_recv()
                far_copy(s3, m3).wait_recv()
                start(w_load(s3, m3))

            if m == 0:
                pl.when(step == 1)(arrange)
            s4, m4 = at(step, m, 4)

            @pl.when((s4 >= 0) & (s4 < sections))
            def _():
                wait(w_load(s4, m4))
                gate(s4, m4)

    def feat_step(n, src, slots):
        return [
            remote(src, slots.at[f], ef_s.at[n, k], ef_r.at[n, k], (r, peer)) for k, peer in enumerate(others)
        ]

    def rows_step(n, src, slots):
        return [
            remote(src, slots.at[r], er_s.at[n, k - 1], er_r.at[n, k - 1], (lax.rem(r + k, rows), f))
            for k in range(1, rows)
        ]

    def sum_all(n, value, src, feat_slots, row_slots, merge):
        feat_slots[f] = value
        src[...] = value
        copies = feat_step(n, src, feat_slots)
        start(copies)
        wait(copies)
        value = merge(feat_slots)
        row_slots[r] = value
        src[...] = value
        copies = rows_step(n, src, row_slots)
        start(copies)
        return copies

    for m in (2, 0, 1):
        start(w_load(sections - 1, m))
    here = pl.ds(pl.multiple_of(f * mine, mine), mine)
    place = lax.broadcasted_iota(jnp.int32, (1, mine), 1) + f * mine
    flat = jnp.where(place < count_ref[0], 1.0, 0.0) * valid_ref[:, here].astype(F32)
    column = jnp.transpose(jnp.broadcast_to(flat, (8, mine)))[:, 0:1]
    wout_buf[...] = jnp.zeros_like(wout_buf)
    wout_buf[0:classes] = wout_ref[...]
    dlog_buf[...] = jnp.zeros_like(dlog_buf)
    dlog_buf[0:classes] = cot_ref[:, here] * flat
    turn[...] = jnp.zeros_like(turn)
    turn[0:1, 0:classes] = bout_ref[...]
    b_out = jnp.transpose(turn[...])[0:TALL, 0:1]
    current = hs[sections]
    count = jnp.sum(column, axis=0, keepdims=True)
    sums = jnp.sum(column * current, axis=0, keepdims=True)
    gap = current - sums / jnp.maximum(count, 1.0)
    square = jnp.sum(column * gap * gap, axis=0, keepdims=True)
    rest = jnp.zeros((ex_a.shape[0] - 2 * blocks - 1, LANES), F32)
    stats = jnp.concatenate(stack(sums) + stack(square) + [jnp.broadcast_to(count, (1, LANES)), rest], axis=0)
    merge = functools.partial(merge_stats, blocks)
    wait(sum_all(0, stats, ex_a, ex_a_feat, ex_a_rows, merge))
    stats = merge(ex_a_rows)
    count = stats[2 * blocks : 2 * blocks + 1, 0:1]
    inv_std = lax.rsqrt(unstack(stats[blocks : 2 * blocks]) / count + 1e-05)
    x_hat[...] = (current - unstack(stats[0:blocks]) / count) * inv_std
    gain, shift = par[4 * sections : 4 * sections + 1], par[4 * sections + 1 : 4 * sections + 2]
    normed = split(x_hat[...] * gain + shift)
    for copy in heads:
        copy.wait_recv()
    w_head = split(whead[...])
    act = dot3(normed, w_head, NN) + bhead_ref[...]
    phi = 0.5 * (1.0 + lax.erf(act * 0.7071067811865476))
    hidden = split(act * phi)
    slope = phi + act * (jnp.exp(-0.5 * act * act) * 0.3989422804014327)
    w_out = split(wout_buf[...])
    logit_buf[f] = (dot3(w_out, hidden, NT) + b_out) * flat
    logit_copies = [
        remote(logit_buf.at[f], logit_buf.at[f], logit_s.at[k], logit_r.at[k], (r, peer))
        for k, peer in enumerate(others)
    ]
    start(logit_copies)
    d_log = dlog_buf[...]
    d_act = dot3(split(d_log), w_out, TN) * slope
    d_act2 = split(d_act)
    d_normed = dot3(d_act2, w_head, NT)
    sums = jnp.concatenate(
        stack(jnp.sum(d_normed * x_hat[...], axis=0, keepdims=True))
        + stack(jnp.sum(d_normed, axis=0, keepdims=True)),
        axis=0,
    )
    dh[...] = d_normed
    copies = sum_all(1, sums, ex_b, ex_b_feat, ex_b_rows, sum_slots)
    vec[...] = jnp.zeros_like(vec)
    hid = act.shape[1]
    aux = 4 * sections
    vec[aux : aux + TALL, 0:hid] = dot3(split(d_log), hidden, NN)
    vec[aux + classes : aux + classes + 1, 0:hid] = jnp.sum(d_act, axis=0, keepdims=True)
    ones = jnp.ones((8, mine), F32)
    vec[aux + classes + 1 : aux + classes + 2, 0:TALL] = dot3(split(ones), split(d_log), NT)[0:1]
    grad = dot3(normed, d_act2, TN)
    for b in range(blocks):
        for t in range(hid // LANES):
            h_grads[b, t * LANES : (t + 1) * LANES] = grad[
                b * LANES : (b + 1) * LANES, t * LANES : (t + 1) * LANES
            ]
    wait(copies)
    sums = sum_slots(ex_b_rows)
    g_gain, g_shift = unstack(sums[0:blocks]), unstack(sums[blocks:])
    dh[...] = inv_std * (dh[...] * gain - column / count * gain * (g_shift + x_hat[...] * g_gain))
    tiny_out[...] = sums
    gin[...] = jnp.zeros_like(gin)

    outs = (go_out, gz_out, gr_out)
    which = (2, 0, 1)
    peers = [(flip(r, 2**k), f) for k in range(levels)]
    piece = depth // cuts
    held, landed = rings(levels)
    z_first = early(levels)

    class Unit:
        def __init__(self, step, j, by_z=False):
            m, cut = j // cuts, j % cuts
            span = pl.ds(cut * piece, piece)
            where = (step % 3) * slots + j
            self.depth = piece
            self.grads = grads.at[(3 * step + m) % 2, :, span]
            self.core, self.total, self.land = core_buf.at[j], total.at[step % held, j], land.at[step % landed, j]
            self.out = outs[m].at[sections - 1 - step, span]
            self.core_sems = [(core_s.at[k, j], core_r.at[k, j]) for k in range(2)]
            self.rs_sems = [(rs_s.at[k, step % landed, j], rs_r.at[k, step % landed, j]) for k in range(levels + 2)]
            self.ag_sems = [(ag_s.at[k, where], ag_r.at[k, where]) for k in range(levels)]
            self.out_sem = out_l.at[where]
            self.plan([1, "y", 0] + list(range(2, levels)) if by_z else ["y"] + list(range(levels)))

        def plan(self, order):
            self.moves, self.backs = [], []
            base, size, block_list, landing, sem = 0, self.depth, [0, 1], 0, 0
            for step in order:
                move = []
                if step == "y":
                    device, sent, kept, from_blocks, block_list = (r, far), base, base, [1], [0]
                else:
                    size //= 2
                    side = (r // 2**step) % 2
                    device, sent, kept, from_blocks = (
                        peers[step], base + (1 - side) * size, base + side * size, block_list,
                    )
                    self.backs.append((device, part(kept, size)))
                for k, block in enumerate(from_blocks):
                    move.append(
                        (device, block, part(sent, size), block_list[k], part(kept, size),
                         pl.ds(landing, size), self.rs_sems[sem])
                    )
                    landing += size
                    sem += 1
                self.moves.append(move)
                base = kept
            self.backs.reverse()

        def core_copies(self):
            return [
                remote(self.grads.at[b], self.core.at[k], *self.core_sems[k], (r, core))
                for k, b in enumerate((core, both))
            ]

        def rs_copies(self, i):
            return [
                remote(self.total.at[block, sent], self.land.at[landing], *sems, device)
                for device, block, sent, _, _, landing, sems in self.moves[i]
            ]

        def add(self, i):
            for _, _, _, block, kept, landing, _ in self.moves[i]:
                self.total[block, kept] += self.land[landing]

        def ag_copy(self, i):
            device, kept = self.backs[i]
            dst = self.out.at[kept]
            return remote(self.total.at[0, kept] if i == 0 else dst, dst, *self.ag_sems[i], device)

        def out_local(self):
            kept = self.backs[0][1]
            return pltpu.make_async_copy(self.total.at[0, kept], self.out.at[kept], self.out_sem)

    class HeadUnit(Unit):
        def __init__(self):
            self.depth = h_grads.shape[1]
            self.grads, self.core, self.total, self.land, self.out = h_grads, h_core, h_total, h_land, ghead_out
            sems = [(hu_s.at[k], hu_r.at[k]) for k in range(2 * levels + 4)]
            self.core_sems, self.rs_sems, self.ag_sems = sems[:2], sems[2 : levels + 4], sems[levels + 4 :]
            self.out_sem = hu_l.at[0]
            self.plan(["y"] + list(range(levels)))

    def stage_core(unit):
        wait(unit.core_copies())
        unit.total[1] = unit.grads[far] + unit.core[1]
        unit.total[0] = unit.grads[f] + unit.core[0]
        start(unit.rs_copies(0))

    def stage_sum(i, unit):
        wait(unit.rs_copies(i))
        unit.add(i)
        if i < levels:
            start(unit.rs_copies(i + 1))
        else:
            unit.ag_copy(0).start()
            unit.out_local().start()

    def stage_out(i, unit):
        if i == 0:
            unit.out_local().wait()
        unit.ag_copy(i).wait()
        if i + 1 < levels:
            unit.ag_copy(i + 1).start()

    stages = [stage_core]
    stages += [functools.partial(stage_sum, i) for i in range(levels + 1)]
    stages += [functools.partial(stage_out, i) for i in range(levels)]

    def outer(m, u, right):
        for t in range(2):
            tile = split(right[:, t * half : (t + 1) * half])
            tile = dot3((upper[0], upper[1]), tile, TN)
            for b in range(half // LANES):
                grads[u % 2, t * (half // LANES) + b] = tile[:, b * LANES : (b + 1) * LANES]

    def back(m, left, t):
        return dot3(left, split(weight[which[m], t * half : (t + 1) * half, :]), NT)

    def compute(step, m):
        s = sections - 1 - step
        u = 3 * step + m
        wait(w_load(s, which[m]))
        h = hs[s]
        if m == 0:
            z, reset, c = zs[s], rs[s], cs[s]
            put(reset * h, low_cols)
            put(x_buf[...] * par[pl.ds(s, 1), :], high_cols)
            d_out = dh[...] * z * (1.0 - c * c)
            vec[pl.ds(2 * sections + s, 1), :] = jnp.sum(d_out, axis=0, keepdims=True)
            outer(m, u, d_out)
            left = split(d_out)
            for t in range(4):
                d_in[:, t * half : (t + 1) * half] = back(m, left, t)
            d_reset[...] = d_in[:, 0:width] * h * reset * (1.0 - reset)
        elif m == 1:
            z, reset, c = zs[s], rs[s], cs[s]
            put(h, low_cols)
            d_up = dh[...] * (c - h) * z * (1.0 - z)
            vec[pl.ds(s, 1), :] = jnp.sum(d_up, axis=0, keepdims=True)
            outer(m, u, d_up)
            dh[...] = dh[...] * (1.0 - z) + d_in[:, 0:width] * reset
            left = split(d_up)
            for t in range(4):
                cols = slice(t % 2 * half, (t % 2 + 1) * half)
                if t < 2:
                    dh[:, cols] += back(m, left, t)
                else:
                    d_in[:, t * half : (t + 1) * half] += back(m, left, t)
        else:
            d_r = d_reset[...]
            vec[pl.ds(sections + s, 1), :] = jnp.sum(d_r, axis=0, keepdims=True)
            outer(m, u, d_r)
            left = split(d_r)
            for t in range(4):
                cols = slice(t % 2 * half, (t % 2 + 1) * half)
                if t < 2:
                    dh[:, cols] += back(m, left, t)
                else:
                    d_xs = d_in[:, t * half : (t + 1) * half] + back(m, left, t)
                    gin[:, cols] += d_xs * par[pl.ds(s, 1), cols]
                    vec[pl.ds(3 * sections + s, 1), cols] = jnp.sum(d_xs * x_buf[:, cols], axis=0, keepdims=True)

        @pl.when(step + 1 < sections)
        def _():
            start(w_load(s - 1, which[m]))

    gf_copies = [
        remote(gin.at[:, lanes(peer)], gfeat_out.at[own_rows], gf_s.at[k], gf_r.at[k], (r, peer))
        for k, peer in enumerate(others)
    ]
    gf_local = pltpu.make_async_copy(gin.at[:, lanes(f)], gfeat_out.at[own_rows], gf_l.at[0])
    vec_feat = [
        remote(ex_c.at[peer], ex_c_feat.at[f], ef_s.at[2, k], ef_r.at[2, k], (r, peer)) for k, peer in enumerate(others)
    ]
    vec_rows = rows_step(2, ex_c_mid, ex_c_rows)
    vec_last = feat_step(3, ex_d, ex_d_feat)
    spread = hid // LANES

    start(HeadUnit().core_copies())

    def before(step, j, back_by):
        u = j - back_by
        return step + u // slots, u % slots

    delays = schedule(levels)

    @pl.loop(0, sections + -(-delays[-1] // slots))
    def _(step):
        for j in range(slots):

            @pl.when(step < sections)
            def _():
                if j % cuts == 0:
                    compute(step, j // cuts)
                start(Unit(step, j).core_copies())

            for delay, stage in zip(delays, stages, strict=True):
                s1, j1 = before(step, j, delay)
                if j1 == slots - 1:

                    @pl.when(s1 == -1)
                    def _():
                        stage(HeadUnit())

                groups = (s1 == 0, (s1 > 0) & (s1 < sections - 1), s1 == sections - 1)
                for by_z in (False, True):
                    active = [g for g, early_units in zip(groups, z_first, strict=True) if (j1 in early_units) == by_z]
                    if active:

                        @pl.when(functools.reduce(jnp.logical_or, active))
                        def _():
                            stage(Unit(s1, j1, by_z))

            if j == 0:

                @pl.when(step == sections)
                def _():
                    for b in range(blocks):
                        ex_c[b, 0:aux] = vec[0:aux, b * LANES : (b + 1) * LANES]
                        ex_c[b, aux : aux + 8] = vec[
                            aux + 8 * (b // spread) : aux + 8 * (b // spread + 1),
                            LANES * (b % spread) : LANES * (b % spread + 1),
                        ]
                    ex_c_feat[f] = ex_c[f]
                    start(vec_feat)
                    gin[...] += dh[...]
                    start(gf_copies + [gf_local])

            if j == 2:

                @pl.when(step == sections)
                def _():
                    wait(vec_feat)
                    ex_c_mid[...] = sum_slots(ex_c_feat)
                    ex_c_rows[r] = ex_c_mid[...]
                    start(vec_rows)

            if j == 5:

                @pl.when(step == sections)
                def _():
                    wait(vec_rows)
                    sums = sum_slots(ex_c_rows)
                    own_out[...] = sums[0:aux]
                    scale = par[0:sections, lanes(f)]
                    inner = jnp.sum(scale * sums[3 * sections : aux], axis=1, keepdims=True) / width
                    ex_d[...] = jnp.zeros_like(ex_d)
                    ex_d[0:sections] = jnp.broadcast_to(inner, (sections, LANES))
                    ex_d[8:16] = sums[aux : aux + 8]
                    ex_d_feat[f] = ex_d[...]
                    start(vec_last)

    wait(vec_last)
    inner = sum_slots(ex_d_feat)[0:sections]
    own_out[3 * sections : aux] = par[0:sections, lanes(f)] * (own_out[3 * sections : aux] - inner)
    for b in range(blocks):
        aux_out[8 * (b // spread) : 8 * (b // spread + 1), LANES * (b % spread) : LANES * (b % spread + 1)] = (
            ex_d_feat[b, 8:16]
        )
    wait(gf_copies + [gf_local])
    wait(logit_copies)
    for b in range(blocks):
        logit_out[:, b * mine : (b + 1) * mine] = logit_buf[b]

    @pl.loop(0, sections)
    def _(s):
        for m in range(3):
            for copy in (y_copy, a_copy, own_copy, x_copy, z_copy, b_copy, c_copy, far_copy):
                copy(s, m).wait_send()

    for copy in firsts + heads:
        copy.wait_send()


def finish_kernel(
    sections, classes,
    gz_ref, gr_ref, go_ref, gfeat_ref, ghead_ref, logit_ref, tiny_ref, own_ref, aux_ref,
    logit_out, gfeat_out, gmask_out, gz_out, gr_out, go_out, bz_out, br_out, bo_out,
    gain_out, shift_out, ghead_out, bhead_out, wout_out, bout_out,
    big, feat, head, load, store,
):
    f = lax.axis_index("feat")
    pairs = [(feat, gfeat_ref, gfeat_out)] + [
        (big.at[m, s], src.at[s], dst.at[s])
        for s in range(sections)
        for m, (src, dst) in enumerate(((gz_ref, gz_out), (gr_ref, gr_out), (go_ref, go_out)))
    ]
    loads = [pltpu.make_async_copy(src, held, load.at[k]) for k, (held, src, _) in enumerate(pairs)]
    stores = [pltpu.make_async_copy(held, dst, store.at[k]) for k, (held, _, dst) in enumerate(pairs)]
    for copy in loads:
        copy.start()
    block = feat.shape[1]
    hidden = bhead_out.shape[1]
    logit_out[...] = logit_ref[0:classes]
    for k, out in enumerate((bz_out, br_out, bo_out, gmask_out)):
        out[...] = own_ref[k * sections : (k + 1) * sections]
    gain_out[...] = tiny_ref[pl.ds(f, 1)]
    shift_out[...] = tiny_ref[pl.ds(tiny_ref.shape[0] // 2 + f, 1)]
    for t in range(hidden // block):
        ghead_out[:, t * block : (t + 1) * block] = ghead_ref[t * block : (t + 1) * block]
    wout_out[...] = aux_ref[0:classes]
    bhead_out[...] = aux_ref[classes : classes + 1]
    bout_out[...] = aux_ref[classes + 1 : classes + 2, 0:classes]
    for load_, store_ in zip(loads, stores, strict=True):
        load_.wait()
        store_.start()
    for copy in stores:
        copy.wait()


def layer(
    rows, groups, features, w_update, w_reset, w_candidate, w_head, counts, validity, mask_logits, b_update, b_reset,
    b_candidate, norm_gain, norm_shift, b_head, w_out, b_out, cotangent,
):
    sections, depth, block = w_update.shape
    width, mine = groups * block, features.shape[0] // groups
    hidden = w_head.shape[1]
    classes = w_out.shape[0]
    units = 3 * sections
    levels = rows.bit_length() - 1
    head_depth = max(hidden, 8 * rows)
    cuts = cuts_of(levels)
    slots = 3 * cuts
    piece = depth // cuts
    held, landed = rings(levels)
    long = 4 * sections + TALL
    sds = jax.ShapeDtypeStruct
    dma = pltpu.SemaphoreType.DMA
    any_, vmem = pl.BlockSpec(memory_space=pl.ANY), pl.BlockSpec(memory_space=pltpu.VMEM)
    grad = sds((sections, depth, block), F32)

    def buf(*shape):
        return pltpu.VMEM(shape, F32)

    made = pl.pallas_call(
        functools.partial(kernel, sections, rows, levels, classes),
        out_shape=[
            grad, grad, grad,
            sds(features.shape, F32),
            sds((head_depth, block), F32),
            sds((TALL, groups * mine), F32),
            sds((2 * groups, block), F32),
            sds((4 * sections, block), F32),
            sds((TALL, hidden), F32),
            sds((sections, 3, groups, depth, block), F32),
        ],
        in_specs=[any_] * 5 + [pl.BlockSpec(memory_space=pltpu.SMEM)] + [vmem] * 11,
        out_specs=[any_] * 5 + [vmem] * 4 + [any_],
        scratch_shapes=[
            buf(mine, width), buf(groups, PAR, block), buf(PAR, width), buf(sections + 1, mine, width),
            buf(sections, mine, width), buf(sections, mine, width), buf(sections, mine, width),
            buf(3, depth, width), pltpu.VMEM((2, mine, depth), BF16),
            buf(width, hidden), buf(mine, width), buf(groups, TALL, mine), buf(mine, width),
            buf(mine, depth), buf(mine, width), buf(mine, width), buf(long, width),
            buf(PAR, block), buf(TALL, hidden), buf(TALL, mine), buf(8, LANES),
            buf(2, groups, depth, block), buf(slots, 2, piece, block), buf(held, slots, 2, piece, block),
            buf(landed, slots, 2 * piece, block),
            buf(groups, head_depth, block), buf(2, head_depth, block), buf(2, head_depth, block),
            buf(2 * head_depth, block),
            buf(16, LANES), buf(groups, 16, LANES), buf(rows, 16, LANES),
            buf(2 * groups, LANES), buf(groups, 2 * groups, LANES), buf(rows, 2 * groups, LANES),
            buf(groups, 4 * sections + 8, block), buf(groups, 4 * sections + 8, block), buf(4 * sections + 8, block),
            buf(rows, 4 * sections + 8, block), buf(16, block), buf(groups, 16, block),
            dma((9,)), dma((9,)), dma((3,)),
        ] + [dma((units,))] * 16 + [
            dma((3, groups)), dma((3,)), dma((3,)), dma((3,)), dma((3,)), dma((1,)),
            dma((4, 3)), dma((4, 3)), dma((3, rows - 1)), dma((3, rows - 1)),
            dma((2, slots)), dma((2, slots)), dma((levels + 2, landed, slots)), dma((levels + 2, landed, slots)),
            dma((levels, 3 * slots)), dma((levels, 3 * slots)), dma((3 * slots,)),
            dma((2 * levels + 4,)), dma((2 * levels + 4,)), dma((1,)),
        ],
        compiler_params=pltpu.CompilerParams(
            collective_id=0, has_side_effects=True, vmem_limit_bytes=62 * 2**20
        ),
    )(
        features, w_update, w_reset, w_candidate, w_head, counts, validity[None], mask_logits, b_update, b_reset,
        b_candidate, norm_gain[None], norm_shift[None], b_head[None], w_out, b_out[None], cotangent,
    )
    row = sds((1, block), F32)
    bias = sds((sections, block), F32)
    return pl.pallas_call(
        functools.partial(finish_kernel, sections, classes),
        out_shape=[
            sds((classes, groups * mine), F32), sds(features.shape, F32), bias, grad, grad, grad, bias, bias, bias,
            row, row, sds((block, hidden), F32), sds((1, hidden), F32), sds((classes, hidden), F32),
            sds((1, classes), F32),
        ],
        in_specs=[any_] * 4 + [vmem] * 5,
        out_specs=[vmem, any_, vmem, any_, any_, any_] + [vmem] * 9,
        scratch_shapes=[
            buf(3, sections, depth, block), buf(*features.shape), buf(8, LANES),
            dma((units + 1,)), dma((units + 1,)),
        ],
        compiler_params=pltpu.CompilerParams(vmem_limit_bytes=62 * 2**20),
    )(*made[:9])


def local(
    rows, groups, features, counts, validity, mask_logits, w_update, w_reset, w_candidate, b_update, b_reset,
    b_candidate, norm_gain, norm_shift, w_head, b_head, w_out, b_out, cotangent,
):
    out = layer(
        rows, groups, features, w_update, w_reset, w_candidate, w_head, counts, validity, mask_logits, b_update,
        b_reset, b_candidate, norm_gain, norm_shift, b_head, w_out.T, b_out, cotangent.T,
    )
    logits, g_feat, g_mask, gz, gr, go, bz, br, bo, gain, shift, g_head, g_b_head, g_w_out, g_b_out = out
    return (
        logits.T, g_feat, g_mask, gz, gr, go, bz, br, bo, gain[0], shift[0], g_head, g_b_head[0], g_w_out.T,
        g_b_out[0],
    )


def solution(mesh):
    rows, groups = mesh.shape["rows"], mesh.shape["feat"]
    split_cols, by_feat = P(None, None, "feat"), P("feat")
    return jax.shard_map(
        functools.partial(local, rows, groups),
        mesh=mesh,
        in_specs=(
            P("rows", "feat"), P("rows"), P("rows"), P(None, "feat"), split_cols, split_cols, split_cols,
            P(None, "feat"), P(None, "feat"), P(None, "feat"), by_feat, by_feat, P("feat", None),
            P(), P(), P(), P("rows", None),
        ),
        out_specs=(
            P("rows", None), P("rows", "feat"), P(None, "feat"), split_cols, split_cols, split_cols,
            P(None, "feat"), P(None, "feat"), P(None, "feat"), by_feat, by_feat, P("feat", None),
            P(), P(), P(),
        ),
        check_vma=False,
    )
```

```python
import functools

import jax
import jax.numpy as jnp
from jax import lax
from jax.experimental import pallas as pl
from jax.experimental.pallas import tpu as pltpu
from jax.sharding import PartitionSpec as P

MESH = pl.DeviceIdType.MESH
F32, BF16 = jnp.float32, jnp.bfloat16
LANES = 128
PAR = 32
TALL = 16
RELAY, CORE, LOAD, GATE = 2, 4, 5, 6


def cuts_of(levels):
    return 4 if levels < 6 else 2


def orders(levels):
    if levels == 3:
        return "EAXAEAXEEAXX", "EXBABXAAAAAA", "BAAABABBXBXB"
    return ("A" * (3 * cuts_of(levels) - 1) + "E",) * 3


def order_of(kind, levels):
    start = {"A": ["y", 0, 1], "E": [1, "y", 0], "B": ["y", 1, 0], "X": [0, "y", 1]}[kind]
    return start + list(range(2, levels))


def schedule(levels):
    if levels == 3:
        return [2, 6, 10, 13, 15, 17, 20, 27]
    return list(range(1, 2 * levels + 3))


def rings(levels):
    return -(-(schedule(levels)[levels + 2] + 1) // (3 * cuts_of(levels))), 2


def flip(index, stride):
    return index + stride - 2 * stride * ((index // stride) % 2)


def split(value):
    high = value.astype(BF16)
    return high, (value - high.astype(F32)).astype(BF16)


def dot3(left, right, dims):
    def one(a, b):
        return lax.dot_general(a, b, (dims, ((), ())), preferred_element_type=F32)

    return one(left[0], right[1]) + one(left[1], right[0]) + one(left[0], right[0])


NN, NT, TN = ((1,), (0,)), ((1,), (1,)), ((0,), (0,))


def remote(src, dst, send, recv, device):
    return pltpu.make_async_remote_copy(
        src_ref=src, dst_ref=dst, send_sem=send, recv_sem=recv, device_id=device, device_id_type=MESH
    )


def meet(devices):
    barrier = pltpu.get_barrier_semaphore()
    for device in devices:
        pl.semaphore_signal(barrier, inc=1, device_id=device, device_id_type=MESH)
    pl.semaphore_wait(barrier, len(devices))


def sum_slots(ref):
    total = ref[0]
    for k in range(1, ref.shape[0]):
        total = total + ref[k]
    return total


def merge_stats(blocks, ref):
    parts = [ref[k] for k in range(ref.shape[0])]
    counts = [p[2 * blocks : 2 * blocks + 1] for p in parts]
    count = functools.reduce(jnp.add, counts)
    sums = functools.reduce(jnp.add, [p[0:blocks] for p in parts])
    mean = sums / jnp.maximum(count, 1.0)
    square = jnp.zeros_like(sums)
    for p, n in zip(parts, counts, strict=True):
        gap = p[0:blocks] / jnp.maximum(n, 1.0) - mean
        square = square + (p[blocks : 2 * blocks] + n * gap * gap)
    rest = ref.shape[1] - 2 * blocks - 1
    return jnp.concatenate([sums, square, count, jnp.zeros((rest, LANES), F32)], axis=0)


def stack(row):
    return [row[:, k * LANES : (k + 1) * LANES] for k in range(row.shape[1] // LANES)]


def unstack(value):
    return jnp.concatenate([value[k : k + 1] for k in range(value.shape[0])], axis=1)


def kernel(
    sections, rows, levels, classes,
    feat_ref, wz_ref, wr_ref, wo_ref, whead_ref, count_ref, valid_ref,
    mask_ref, bz_ref, br_ref, bo_ref, gain_ref, shift_ref, bhead_ref, wout_ref, bout_ref, cot_ref,
    gz_out, gr_out, go_out, gfeat_out, ghead_out, logit_out, tiny_out, own_out, aux_out, wfull,
    x_buf, small_buf, par, hs, zs, rs, cs, weight, upper,
    whead, x_hat, logit_buf, dh, d_in, d_reset, gin, vec,
    small_ref, wout_buf, dlog_buf, turn,
    grads, core_buf, total, land,
    h_grads, h_core, h_total, h_land,
    ex_a, ex_a_feat, ex_a_rows, ex_b, ex_b_feat, ex_b_rows,
    ex_c, ex_c_feat, ex_c_mid, ex_c_rows, ex_d, ex_d_feat,
    first_s, first_r, first_l, fy_s, fy_r, a_s, a_r, x_s, x_r, z_s, z_r, b_s, b_r, c_s, c_r,
    own_s, own_r, far_s, far_r, load_w, logit_s, logit_r, gf_s, gf_r, gf_l,
    ef_s, ef_r, er_s, er_r,
    core_s, core_r, rs_s, rs_r, ag_s, ag_r, out_l, hu_s, hu_r, hu_l,
):
    r, f = lax.axis_index("rows"), lax.axis_index("feat")
    weights = (wz_ref, wr_ref, wo_ref)
    units = 3 * sections
    depth = wz_ref.shape[1]
    cuts = cuts_of(levels)
    slots = 3 * cuts
    mine, width = x_buf.shape
    blocks = small_buf.shape[0]
    half = width // 2
    core, far, both = flip(f, 1), flip(f, 2), flip(flip(f, 1), 2)
    others = (core, far, both)
    rx, rz = flip(r, 1), flip(r, 2)
    quarter = depth // 4
    cut_b, cut_c = 3 * quarter // 8, 3 * quarter // 8 + 5 * quarter // 16
    q = 2 * (r % 2) + (r // 2) % 2
    q_x, q_z, q_d = flip(q, 2), flip(q, 1), flip(flip(q, 1), 2)

    def lanes(index):
        return pl.ds(pl.multiple_of(index * LANES, LANES), LANES)

    def part(start, size):
        return pl.ds(pl.multiple_of(start, 8), size)

    def rows_of(index, start, size):
        return part(index * quarter + start, size)

    meet([(r, peer) for peer in others] + [(lax.rem(r + k, rows), f) for k in range(1, rows)])

    small_ref[...] = jnp.zeros_like(small_ref)
    for k, ref in enumerate((mask_ref, bz_ref, br_ref, bo_ref)):
        small_ref[k * sections : (k + 1) * sections] = ref[...]
    small_ref[4 * sections : 4 * sections + 1] = gain_ref[...]
    small_ref[4 * sections + 1 : 4 * sections + 2] = shift_ref[...]
    own_rows = pl.ds(pl.multiple_of(f * mine, mine), mine)
    firsts, heads = [], []
    for k, peer in enumerate(others):
        chunk = pl.ds(pl.multiple_of(peer * mine, mine), mine)
        firsts += [
            remote(small_ref, small_buf.at[f], first_s.at[k], first_r.at[k], (r, peer)),
            remote(feat_ref.at[chunk], x_buf.at[:, lanes(f)], first_s.at[3 + k], first_r.at[3 + k], (r, peer)),
        ]
        heads.append(remote(whead_ref, whead.at[lanes(f)], first_s.at[6 + k], first_r.at[6 + k], (r, peer)))
    locals_ = [
        pltpu.make_async_copy(small_ref, small_buf.at[f], first_l.at[0]),
        pltpu.make_async_copy(feat_ref.at[own_rows], x_buf.at[:, lanes(f)], first_l.at[1]),
        pltpu.make_async_copy(whead_ref, whead.at[lanes(f)], first_l.at[2]),
    ]

    def y_copy(s, m):
        u, span = 3 * s + m, rows_of(q, 0, quarter)
        return remote(weights[m].at[s, span], wfull.at[s, m, f, span], fy_s.at[u], fy_r.at[u], (r, far))

    def a_copy(s, m):
        u, span = 3 * s + m, rows_of(q_d, 0, cut_b)
        return remote(weights[m].at[s, span], wfull.at[s, m, f, span], a_s.at[u], a_r.at[u], (r, far))

    def own_copy(s, m):
        u = 3 * s + m
        return remote(weights[m].at[s], wfull.at[s, m, f], own_s.at[u], own_r.at[u], (r, core))

    def pass_on(s, m, span, send, recv, device):
        u, ref = 3 * s + m, wfull.at[s, m, far, span]
        return remote(ref, ref, send.at[u], recv.at[u], device)

    def x_copy(s, m):
        return pass_on(s, m, rows_of(q, 0, quarter), x_s, x_r, (rx, f))

    def z_copy(s, m):
        return pass_on(s, m, rows_of(q, 0, quarter), z_s, z_r, (rz, f))

    def b_copy(s, m):
        return pass_on(s, m, rows_of(q_z, cut_b, cut_c - cut_b), b_s, b_r, (rx, f))

    def c_copy(s, m):
        return pass_on(s, m, rows_of(q_x, cut_c, quarter - cut_c), c_s, c_r, (rz, f))

    def far_copy(s, m):
        u, ref = 3 * s + m, wfull.at[s, m, far]
        return remote(ref, ref, far_s.at[u], far_r.at[u], (r, core))

    def w_load(s, m):
        copies = [pltpu.make_async_copy(weights[m].at[s], weight.at[m, :, lanes(f)], load_w.at[m, 0])]
        for k, b in enumerate(others):
            copies.append(
                pltpu.make_async_copy(wfull.at[s, m, b], weight.at[m, :, lanes(b)], load_w.at[m, 1 + k])
            )
        return copies

    def start(copies):
        for copy in copies:
            copy.start()

    def wait(copies):
        for copy in copies:
            copy.wait()

    def send_own(s):
        for m in range(3):
            y_copy(s, m).start()
            a_copy(s, m).start()
            own_copy(s, m).start()

    send_own(0)
    start(firsts + locals_)

    @pl.loop(1, sections)
    def _(s):
        send_own(s)

    start(heads)

    def arrange():
        for copy in firsts:
            copy.wait_recv()
        wait(locals_)
        par[...] = jnp.concatenate([small_buf[b] for b in range(blocks)], axis=1)
        logits = par[0:8]
        probs = jnp.exp(logits - jnp.max(logits, axis=1, keepdims=True))
        probs = probs / jnp.sum(probs, axis=1, keepdims=True)
        par[0:sections] = (width * probs)[0:sections]
        hs[0] = x_buf[...]

    def put(value, at_rows):
        for k, piece in enumerate(split(value)):
            upper[k, :, at_rows] = piece

    low_cols, high_cols = slice(0, width), slice(width, 2 * width)

    def product(s, m):
        tiles = []
        for t in range(2):
            w = split(weight[m, :, t * half : (t + 1) * half])
            tiles.append(dot3((upper[0], upper[1]), w, NN))
        return jnp.concatenate(tiles, axis=1) + par[pl.ds(sections * (m + 1) + s, 1), :]

    def gate(s, m):
        if m == 0:
            put(hs[s], low_cols)
            put(x_buf[...] * par[pl.ds(s, 1), :], high_cols)
            zs[s] = jax.nn.sigmoid(product(s, 0))
        elif m == 1:
            rs[s] = jax.nn.sigmoid(product(s, 1))
            put(rs[s] * hs[s], low_cols)
        else:
            cand = jnp.tanh(product(s, 2))
            cs[s] = cand
            hs[s + 1] = hs[s] + zs[s] * (cand - hs[s])

    def at(step, m, back_by):
        u = m - back_by
        return step + u // 3, u % 3

    @pl.loop(0, sections + -(-GATE // 3))
    def _(step):
        for m in range(3):

            @pl.when(step < sections)
            def _():
                y_copy(step, m).wait_recv()
                x_copy(step, m).start()
                z_copy(step, m).start()

            s1, m1 = at(step, m, RELAY)

            @pl.when((s1 >= 0) & (s1 < sections))
            def _():
                x_copy(s1, m1).wait_recv()
                z_copy(s1, m1).wait_recv()
                b_copy(s1, m1).start()
                c_copy(s1, m1).start()

            s2, m2 = at(step, m, CORE)

            @pl.when((s2 >= 0) & (s2 < sections))
            def _():
                a_copy(s2, m2).wait_recv()
                b_copy(s2, m2).wait_recv()
                c_copy(s2, m2).wait_recv()
                far_copy(s2, m2).start()

            s3, m3 = at(step, m, LOAD)

            @pl.when((s3 >= 0) & (s3 < sections))
            def _():
                own_copy(s3, m3).wait_recv()
                far_copy(s3, m3).wait_recv()
                start(w_load(s3, m3))

            if m == LOAD % 3:
                pl.when(step == LOAD // 3)(arrange)
            s4, m4 = at(step, m, GATE)

            @pl.when((s4 >= 0) & (s4 < sections))
            def _():
                wait(w_load(s4, m4))
                gate(s4, m4)

    def feat_step(n, src, slots):
        return [
            remote(src, slots.at[f], ef_s.at[n, k], ef_r.at[n, k], (r, peer)) for k, peer in enumerate(others)
        ]

    def rows_step(n, src, slots):
        return [
            remote(src, slots.at[r], er_s.at[n, k - 1], er_r.at[n, k - 1], (lax.rem(r + k, rows), f))
            for k in range(1, rows)
        ]

    def sum_all(n, value, src, feat_slots, row_slots, merge):
        feat_slots[f] = value
        src[...] = value
        copies = feat_step(n, src, feat_slots)
        start(copies)
        wait(copies)
        value = merge(feat_slots)
        row_slots[r] = value
        src[...] = value
        copies = rows_step(n, src, row_slots)
        start(copies)
        return copies

    for m in (2, 0, 1):
        start(w_load(sections - 1, m))
    here = pl.ds(pl.multiple_of(f * mine, mine), mine)
    place = lax.broadcasted_iota(jnp.int32, (1, mine), 1) + f * mine
    flat = jnp.where(place < count_ref[0], 1.0, 0.0) * valid_ref[:, here].astype(F32)
    column = jnp.transpose(jnp.broadcast_to(flat, (8, mine)))[:, 0:1]
    wout_buf[...] = jnp.zeros_like(wout_buf)
    wout_buf[0:classes] = wout_ref[...]
    dlog_buf[...] = jnp.zeros_like(dlog_buf)
    dlog_buf[0:classes] = cot_ref[:, here] * flat
    turn[...] = jnp.zeros_like(turn)
    turn[0:1, 0:classes] = bout_ref[...]
    b_out = jnp.transpose(turn[...])[0:TALL, 0:1]
    current = hs[sections]
    count = jnp.sum(column, axis=0, keepdims=True)
    sums = jnp.sum(column * current, axis=0, keepdims=True)
    gap = current - sums / jnp.maximum(count, 1.0)
    square = jnp.sum(column * gap * gap, axis=0, keepdims=True)
    rest = jnp.zeros((ex_a.shape[0] - 2 * blocks - 1, LANES), F32)
    stats = jnp.concatenate(stack(sums) + stack(square) + [jnp.broadcast_to(count, (1, LANES)), rest], axis=0)
    merge = functools.partial(merge_stats, blocks)
    wait(sum_all(0, stats, ex_a, ex_a_feat, ex_a_rows, merge))
    stats = merge(ex_a_rows)
    count = stats[2 * blocks : 2 * blocks + 1, 0:1]
    inv_std = lax.rsqrt(unstack(stats[blocks : 2 * blocks]) / count + 1e-05)
    x_hat[...] = (current - unstack(stats[0:blocks]) / count) * inv_std
    gain, shift = par[4 * sections : 4 * sections + 1], par[4 * sections + 1 : 4 * sections + 2]
    normed = split(x_hat[...] * gain + shift)
    for copy in heads:
        copy.wait_recv()
    w_head = split(whead[...])
    act = dot3(normed, w_head, NN) + bhead_ref[...]
    phi = 0.5 * (1.0 + lax.erf(act * 0.7071067811865476))
    hidden = split(act * phi)
    slope = phi + act * (jnp.exp(-0.5 * act * act) * 0.3989422804014327)
    w_out = split(wout_buf[...])
    logit_buf[f] = (dot3(w_out, hidden, NT) + b_out) * flat
    logit_copies = [
        remote(logit_buf.at[f], logit_buf.at[f], logit_s.at[k], logit_r.at[k], (r, peer))
        for k, peer in enumerate(others)
    ]
    start(logit_copies)
    d_log = dlog_buf[...]
    d_act = dot3(split(d_log), w_out, TN) * slope
    d_act2 = split(d_act)
    d_normed = dot3(d_act2, w_head, NT)
    sums = jnp.concatenate(
        stack(jnp.sum(d_normed * x_hat[...], axis=0, keepdims=True))
        + stack(jnp.sum(d_normed, axis=0, keepdims=True)),
        axis=0,
    )
    dh[...] = d_normed
    copies = sum_all(1, sums, ex_b, ex_b_feat, ex_b_rows, sum_slots)
    vec[...] = jnp.zeros_like(vec)
    hid = act.shape[1]
    aux = 4 * sections
    vec[aux : aux + TALL, 0:hid] = dot3(split(d_log), hidden, NN)
    vec[aux + classes : aux + classes + 1, 0:hid] = jnp.sum(d_act, axis=0, keepdims=True)
    ones = jnp.ones((8, mine), F32)
    vec[aux + classes + 1 : aux + classes + 2, 0:TALL] = dot3(split(ones), split(d_log), NT)[0:1]
    grad = dot3(normed, d_act2, TN)
    for b in range(blocks):
        for t in range(hid // LANES):
            h_grads[b, t * LANES : (t + 1) * LANES] = grad[
                b * LANES : (b + 1) * LANES, t * LANES : (t + 1) * LANES
            ]
    wait(copies)
    sums = sum_slots(ex_b_rows)
    g_gain, g_shift = unstack(sums[0:blocks]), unstack(sums[blocks:])
    dh[...] = inv_std * (dh[...] * gain - column / count * gain * (g_shift + x_hat[...] * g_gain))
    tiny_out[...] = sums
    gin[...] = jnp.zeros_like(gin)

    outs = (go_out, gz_out, gr_out)
    which = (2, 0, 1)
    peers = [(flip(r, 2**k), f) for k in range(levels)]
    piece = depth // cuts
    held, landed = rings(levels)
    kinds = orders(levels)

    class Unit:
        def __init__(self, step, j, kind="A"):
            m, cut = j // cuts, j % cuts
            span = pl.ds(cut * piece, piece)
            where = (step % 3) * slots + j
            self.depth = piece
            self.grads = grads.at[(3 * step + m) % 2, :, span]
            self.core, self.total, self.land = core_buf.at[j], total.at[step % held, j], land.at[step % landed, j]
            self.out = outs[m].at[sections - 1 - step, span]
            self.core_sems = [(core_s.at[k, j], core_r.at[k, j]) for k in range(2)]
            self.rs_sems = [(rs_s.at[k, step % landed, j], rs_r.at[k, step % landed, j]) for k in range(levels + 2)]
            self.ag_sems = [(ag_s.at[k, where], ag_r.at[k, where]) for k in range(levels)]
            self.out_sem = out_l.at[where]
            self.plan(order_of(kind, levels))

        def plan(self, order):
            self.moves, self.backs = [], []
            base, size, block_list, landing, sem = 0, self.depth, [0, 1], 0, 0
            for step in order:
                move = []
                if step == "y":
                    device, sent, kept, from_blocks, block_list = (r, far), base, base, [1], [0]
                else:
                    size //= 2
                    side = (r // 2**step) % 2
                    device, sent, kept, from_blocks = (
                        peers[step], base + (1 - side) * size, base + side * size, block_list,
                    )
                    self.backs.append((device, part(kept, size)))
                for k, block in enumerate(from_blocks):
                    move.append(
                        (device, block, part(sent, size), block_list[k], part(kept, size),
                         pl.ds(landing, size), self.rs_sems[sem])
                    )
                    landing += size
                    sem += 1
                self.moves.append(move)
                base = kept
            self.backs.reverse()

        def core_copies(self):
            return [
                remote(self.grads.at[b], self.core.at[k], *self.core_sems[k], (r, core))
                for k, b in enumerate((core, both))
            ]

        def rs_copies(self, i):
            return [
                remote(self.total.at[block, sent], self.land.at[landing], *sems, device)
                for device, block, sent, _, _, landing, sems in self.moves[i]
            ]

        def add(self, i):
            for _, _, _, block, kept, landing, _ in self.moves[i]:
                self.total[block, kept] += self.land[landing]

        def ag_copy(self, i):
            device, kept = self.backs[i]
            dst = self.out.at[kept]
            return remote(self.total.at[0, kept] if i == 0 else dst, dst, *self.ag_sems[i], device)

        def out_local(self):
            kept = self.backs[0][1]
            return pltpu.make_async_copy(self.total.at[0, kept], self.out.at[kept], self.out_sem)

    class HeadUnit(Unit):
        def __init__(self):
            self.depth = h_grads.shape[1]
            self.grads, self.core, self.total, self.land, self.out = h_grads, h_core, h_total, h_land, ghead_out
            sems = [(hu_s.at[k], hu_r.at[k]) for k in range(2 * levels + 4)]
            self.core_sems, self.rs_sems, self.ag_sems = sems[:2], sems[2 : levels + 4], sems[levels + 4 :]
            self.out_sem = hu_l.at[0]
            self.plan(order_of("A", levels))

    def stage_core(unit):
        wait(unit.core_copies())
        unit.total[1] = unit.grads[far] + unit.core[1]
        unit.total[0] = unit.grads[f] + unit.core[0]
        start(unit.rs_copies(0))

    def stage_sum(i, unit):
        wait(unit.rs_copies(i))
        unit.add(i)
        if i < levels:
            start(unit.rs_copies(i + 1))
        else:
            unit.ag_copy(0).start()
            unit.out_local().start()

    def stage_out(i, unit):
        if i == 0:
            unit.out_local().wait()
        unit.ag_copy(i).wait()
        if i + 1 < levels:
            unit.ag_copy(i + 1).start()

    stages = [stage_core]
    stages += [functools.partial(stage_sum, i) for i in range(levels + 1)]
    stages += [functools.partial(stage_out, i) for i in range(levels)]

    def outer(m, u, right):
        for t in range(2):
            tile = split(right[:, t * half : (t + 1) * half])
            tile = dot3((upper[0], upper[1]), tile, TN)
            for b in range(half // LANES):
                grads[u % 2, t * (half // LANES) + b] = tile[:, b * LANES : (b + 1) * LANES]

    def back(m, left, t):
        return dot3(left, split(weight[which[m], t * half : (t + 1) * half, :]), NT)

    def compute(step, m):
        s = sections - 1 - step
        u = 3 * step + m
        wait(w_load(s, which[m]))
        h = hs[s]
        if m == 0:
            z, reset, c = zs[s], rs[s], cs[s]
            put(reset * h, low_cols)
            put(x_buf[...] * par[pl.ds(s, 1), :], high_cols)
            d_out = dh[...] * z * (1.0 - c * c)
            vec[pl.ds(2 * sections + s, 1), :] = jnp.sum(d_out, axis=0, keepdims=True)
            outer(m, u, d_out)
            left = split(d_out)
            for t in range(4):
                d_in[:, t * half : (t + 1) * half] = back(m, left, t)
            d_reset[...] = d_in[:, 0:width] * h * reset * (1.0 - reset)
        elif m == 1:
            z, reset, c = zs[s], rs[s], cs[s]
            put(h, low_cols)
            d_up = dh[...] * (c - h) * z * (1.0 - z)
            vec[pl.ds(s, 1), :] = jnp.sum(d_up, axis=0, keepdims=True)
            outer(m, u, d_up)
            dh[...] = dh[...] * (1.0 - z) + d_in[:, 0:width] * reset
            left = split(d_up)
            for t in range(4):
                cols = slice(t % 2 * half, (t % 2 + 1) * half)
                if t < 2:
                    dh[:, cols] += back(m, left, t)
                else:
                    d_in[:, t * half : (t + 1) * half] += back(m, left, t)
        else:
            d_r = d_reset[...]
            vec[pl.ds(sections + s, 1), :] = jnp.sum(d_r, axis=0, keepdims=True)
            outer(m, u, d_r)
            left = split(d_r)
            for t in range(4):
                cols = slice(t % 2 * half, (t % 2 + 1) * half)
                if t < 2:
                    dh[:, cols] += back(m, left, t)
                else:
                    d_xs = d_in[:, t * half : (t + 1) * half] + back(m, left, t)
                    gin[:, cols] += d_xs * par[pl.ds(s, 1), cols]
                    vec[pl.ds(3 * sections + s, 1), cols] = jnp.sum(d_xs * x_buf[:, cols], axis=0, keepdims=True)

        @pl.when(step + 1 < sections)
        def _():
            start(w_load(s - 1, which[m]))

    gf_copies = [
        remote(gin.at[:, lanes(peer)], gfeat_out.at[own_rows], gf_s.at[k], gf_r.at[k], (r, peer))
        for k, peer in enumerate(others)
    ]
    gf_local = pltpu.make_async_copy(gin.at[:, lanes(f)], gfeat_out.at[own_rows], gf_l.at[0])
    vec_feat = [
        remote(ex_c.at[peer], ex_c_feat.at[f], ef_s.at[2, k], ef_r.at[2, k], (r, peer)) for k, peer in enumerate(others)
    ]
    vec_rows = rows_step(2, ex_c_mid, ex_c_rows)
    vec_last = feat_step(3, ex_d, ex_d_feat)
    spread = hid // LANES

    start(HeadUnit().core_copies())

    def before(step, j, back_by):
        u = j - back_by
        return step + u // slots, u % slots

    delays = schedule(levels)

    @pl.loop(0, sections + -(-delays[-1] // slots))
    def _(step):
        for j in range(slots):

            @pl.when(step < sections)
            def _():
                if j % cuts == 0:
                    compute(step, j // cuts)
                start(Unit(step, j).core_copies())

            for delay, stage in zip(delays, stages, strict=True):
                s1, j1 = before(step, j, delay)
                if j1 == slots - 1:

                    @pl.when(s1 == -1)
                    def _():
                        stage(HeadUnit())

                groups = (s1 == 0, (s1 > 0) & (s1 < sections - 1), s1 == sections - 1)
                for kind in sorted({row[j1] for row in kinds}):
                    active = [g for g, row in zip(groups, kinds, strict=True) if row[j1] == kind]

                    @pl.when(functools.reduce(jnp.logical_or, active))
                    def _():
                        stage(Unit(s1, j1, kind))

            if j == 0:

                @pl.when(step == sections)
                def _():
                    for b in range(blocks):
                        ex_c[b, 0:aux] = vec[0:aux, b * LANES : (b + 1) * LANES]
                        ex_c[b, aux : aux + 8] = vec[
                            aux + 8 * (b // spread) : aux + 8 * (b // spread + 1),
                            LANES * (b % spread) : LANES * (b % spread + 1),
                        ]
                    ex_c_feat[f] = ex_c[f]
                    start(vec_feat)
                    gin[...] += dh[...]
                    start(gf_copies + [gf_local])

            if j == 2:

                @pl.when(step == sections)
                def _():
                    wait(vec_feat)
                    ex_c_mid[...] = sum_slots(ex_c_feat)
                    ex_c_rows[r] = ex_c_mid[...]
                    start(vec_rows)

            if j == 5:

                @pl.when(step == sections)
                def _():
                    wait(vec_rows)
                    sums = sum_slots(ex_c_rows)
                    own_out[...] = sums[0:aux]
                    scale = par[0:sections, lanes(f)]
                    inner = jnp.sum(scale * sums[3 * sections : aux], axis=1, keepdims=True) / width
                    ex_d[...] = jnp.zeros_like(ex_d)
                    ex_d[0:sections] = jnp.broadcast_to(inner, (sections, LANES))
                    ex_d[8:16] = sums[aux : aux + 8]
                    ex_d_feat[f] = ex_d[...]
                    start(vec_last)

    wait(vec_last)
    inner = sum_slots(ex_d_feat)[0:sections]
    own_out[3 * sections : aux] = par[0:sections, lanes(f)] * (own_out[3 * sections : aux] - inner)
    for b in range(blocks):
        aux_out[8 * (b // spread) : 8 * (b // spread + 1), LANES * (b % spread) : LANES * (b % spread + 1)] = (
            ex_d_feat[b, 8:16]
        )
    wait(gf_copies + [gf_local])
    wait(logit_copies)
    for b in range(blocks):
        logit_out[:, b * mine : (b + 1) * mine] = logit_buf[b]

    @pl.loop(0, sections)
    def _(s):
        for m in range(3):
            for copy in (y_copy, a_copy, own_copy, x_copy, z_copy, b_copy, c_copy, far_copy):
                copy(s, m).wait_send()

    for copy in firsts + heads:
        copy.wait_send()


def finish_kernel(
    sections, classes,
    gz_ref, gr_ref, go_ref, gfeat_ref, ghead_ref, logit_ref, tiny_ref, own_ref, aux_ref,
    logit_out, gfeat_out, gmask_out, gz_out, gr_out, go_out, bz_out, br_out, bo_out,
    gain_out, shift_out, ghead_out, bhead_out, wout_out, bout_out,
    store,
):
    f = lax.axis_index("feat")
    pairs = [(gfeat_ref, gfeat_out)] + [
        (src.at[s], dst.at[s])
        for s in range(sections)
        for src, dst in ((gz_ref, gz_out), (gr_ref, gr_out), (go_ref, go_out))
    ]
    stores = [pltpu.make_async_copy(src, dst, store.at[k]) for k, (src, dst) in enumerate(pairs)]
    for copy in stores:
        copy.start()
    block = gfeat_ref.shape[1]
    hidden = bhead_out.shape[1]
    logit_out[...] = logit_ref[0:classes]
    for k, out in enumerate((bz_out, br_out, bo_out, gmask_out)):
        out[...] = own_ref[k * sections : (k + 1) * sections]
    gain_out[...] = tiny_ref[pl.ds(f, 1)]
    shift_out[...] = tiny_ref[pl.ds(tiny_ref.shape[0] // 2 + f, 1)]
    for t in range(hidden // block):
        ghead_out[:, t * block : (t + 1) * block] = ghead_ref[t * block : (t + 1) * block]
    wout_out[...] = aux_ref[0:classes]
    bhead_out[...] = aux_ref[classes : classes + 1]
    bout_out[...] = aux_ref[classes + 1 : classes + 2, 0:classes]
    for copy in stores:
        copy.wait()


def layer(
    rows, groups, features, w_update, w_reset, w_candidate, w_head, counts, validity, mask_logits, b_update, b_reset,
    b_candidate, norm_gain, norm_shift, b_head, w_out, b_out, cotangent,
):
    sections, depth, block = w_update.shape
    width, mine = groups * block, features.shape[0] // groups
    hidden = w_head.shape[1]
    classes = w_out.shape[0]
    units = 3 * sections
    levels = rows.bit_length() - 1
    head_depth = max(hidden, 8 * rows)
    cuts = cuts_of(levels)
    slots = 3 * cuts
    piece = depth // cuts
    held, landed = rings(levels)
    long = 4 * sections + TALL
    sds = jax.ShapeDtypeStruct
    dma = pltpu.SemaphoreType.DMA
    any_, vmem = pl.BlockSpec(memory_space=pl.ANY), pl.BlockSpec(memory_space=pltpu.VMEM)
    grad = sds((sections, depth, block), F32)
    held_grad = pltpu.VMEM((sections, depth, block), F32)

    def buf(*shape):
        return pltpu.VMEM(shape, F32)

    made = pl.pallas_call(
        functools.partial(kernel, sections, rows, levels, classes),
        out_shape=[
            held_grad, held_grad, held_grad,
            pltpu.VMEM(features.shape, F32),
            pltpu.VMEM((head_depth, block), F32),
            pltpu.VMEM((TALL, groups * mine), F32),
            pltpu.VMEM((2 * groups, block), F32),
            pltpu.VMEM((4 * sections, block), F32),
            pltpu.VMEM((TALL, hidden), F32),
            sds((sections, 3, groups, depth, block), F32),
        ],
        in_specs=[any_] * 5 + [pl.BlockSpec(memory_space=pltpu.SMEM)] + [vmem] * 11,
        out_specs=[vmem] * 9 + [any_],
        scratch_shapes=[
            buf(mine, width), buf(groups, PAR, block), buf(PAR, width), buf(sections + 1, mine, width),
            buf(sections, mine, width), buf(sections, mine, width), buf(sections, mine, width),
            buf(3, depth, width), pltpu.VMEM((2, mine, depth), BF16),
            buf(width, hidden), buf(mine, width), buf(groups, TALL, mine), buf(mine, width),
            buf(mine, depth), buf(mine, width), buf(mine, width), buf(long, width),
            buf(PAR, block), buf(TALL, hidden), buf(TALL, mine), buf(8, LANES),
            buf(2, groups, depth, block), buf(slots, 2, piece, block), buf(held, slots, 2, piece, block),
            buf(landed, slots, 2 * piece, block),
            buf(groups, head_depth, block), buf(2, head_depth, block), buf(2, head_depth, block),
            buf(2 * head_depth, block),
            buf(16, LANES), buf(groups, 16, LANES), buf(rows, 16, LANES),
            buf(2 * groups, LANES), buf(groups, 2 * groups, LANES), buf(rows, 2 * groups, LANES),
            buf(groups, 4 * sections + 8, block), buf(groups, 4 * sections + 8, block), buf(4 * sections + 8, block),
            buf(rows, 4 * sections + 8, block), buf(16, block), buf(groups, 16, block),
            dma((9,)), dma((9,)), dma((3,)),
        ] + [dma((units,))] * 16 + [
            dma((3, groups)), dma((3,)), dma((3,)), dma((3,)), dma((3,)), dma((1,)),
            dma((4, 3)), dma((4, 3)), dma((3, rows - 1)), dma((3, rows - 1)),
            dma((2, slots)), dma((2, slots)), dma((levels + 2, landed, slots)), dma((levels + 2, landed, slots)),
            dma((levels, 3 * slots)), dma((levels, 3 * slots)), dma((3 * slots,)),
            dma((2 * levels + 4,)), dma((2 * levels + 4,)), dma((1,)),
        ],
        compiler_params=pltpu.CompilerParams(
            collective_id=0, has_side_effects=True, vmem_limit_bytes=52 * 2**20
        ),
    )(
        features, w_update, w_reset, w_candidate, w_head, counts, validity[None], mask_logits, b_update, b_reset,
        b_candidate, norm_gain[None], norm_shift[None], b_head[None], w_out, b_out[None], cotangent,
    )
    row = sds((1, block), F32)
    bias = sds((sections, block), F32)
    return pl.pallas_call(
        functools.partial(finish_kernel, sections, classes),
        out_shape=[
            sds((classes, groups * mine), F32), sds(features.shape, F32), bias, grad, grad, grad, bias, bias, bias,
            row, row, sds((block, hidden), F32), sds((1, hidden), F32), sds((classes, hidden), F32),
            sds((1, classes), F32),
        ],
        in_specs=[vmem] * 3 + [vmem] + [vmem] * 5,
        out_specs=[vmem, any_, vmem, any_, any_, any_] + [vmem] * 9,
        scratch_shapes=[dma((units + 1,))],
        compiler_params=pltpu.CompilerParams(vmem_limit_bytes=16 * 2**20),
    )(*made[:9])


def local(
    rows, groups, features, counts, validity, mask_logits, w_update, w_reset, w_candidate, b_update, b_reset,
    b_candidate, norm_gain, norm_shift, w_head, b_head, w_out, b_out, cotangent,
):
    out = layer(
        rows, groups, features, w_update, w_reset, w_candidate, w_head, counts, validity, mask_logits, b_update,
        b_reset, b_candidate, norm_gain, norm_shift, b_head, w_out.T, b_out, cotangent.T,
    )
    logits, g_feat, g_mask, gz, gr, go, bz, br, bo, gain, shift, g_head, g_b_head, g_w_out, g_b_out = out
    return (
        logits.T, g_feat, g_mask, gz, gr, go, bz, br, bo, gain[0], shift[0], g_head, g_b_head[0], g_w_out.T,
        g_b_out[0],
    )


def solution(mesh):
    rows, groups = mesh.shape["rows"], mesh.shape["feat"]
    split_cols, by_feat = P(None, None, "feat"), P("feat")
    return jax.shard_map(
        functools.partial(local, rows, groups),
        mesh=mesh,
        in_specs=(
            P("rows", "feat"), P("rows"), P("rows"), P(None, "feat"), split_cols, split_cols, split_cols,
            P(None, "feat"), P(None, "feat"), P(None, "feat"), by_feat, by_feat, P("feat", None),
            P(), P(), P(), P("rows", None),
        ),
        out_specs=(
            P("rows", None), P("rows", "feat"), P(None, "feat"), split_cols, split_cols, split_cols,
            P(None, "feat"), P(None, "feat"), P(None, "feat"), by_feat, by_feat, P("feat", None),
            P(), P(), P(),
        ),
        check_vma=False,
    )
```

```python
import functools

import jax
import jax.numpy as jnp
from jax import lax
from jax.experimental import pallas as pl
from jax.experimental.pallas import tpu as pltpu
from jax.sharding import PartitionSpec as P

MESH = pl.DeviceIdType.MESH
F32, BF16 = jnp.float32, jnp.bfloat16
LANES = 128
PAR = 32
TALL = 16
RELAY, CORE, LOAD, GATE = 1, 3, 4, 5


def cuts_of(levels):
    return 4 if levels < 6 else 2


def orders(levels):
    if levels == 3:
        return "EAXAEAXEEAXX", "EXBABXAAAAAA", "BAAABABBXBXB"
    return ("A" * (3 * cuts_of(levels) - 1) + "E",) * 3


def order_of(kind, levels):
    start = {"A": ["y", 0, 1], "E": [1, "y", 0], "B": ["y", 1, 0], "X": [0, "y", 1]}[kind]
    return start + list(range(2, levels))


def schedule(levels):
    if levels == 3:
        return [3, 7, 11, 14, 16, 18, 21, 28]
    return list(range(1, 2 * levels + 3))


def rings(levels):
    return -(-(schedule(levels)[levels + 2] + 1) // (3 * cuts_of(levels))), 2


def flip(index, stride):
    return index + stride - 2 * stride * ((index // stride) % 2)


def split(value):
    high = value.astype(BF16)
    return high, (value - high.astype(F32)).astype(BF16)


def dot3(left, right, dims):
    def one(a, b):
        return lax.dot_general(a, b, (dims, ((), ())), preferred_element_type=F32)

    return one(left[0], right[1]) + one(left[1], right[0]) + one(left[0], right[0])


NN, NT, TN = ((1,), (0,)), ((1,), (1,)), ((0,), (0,))


def remote(src, dst, send, recv, device):
    return pltpu.make_async_remote_copy(
        src_ref=src, dst_ref=dst, send_sem=send, recv_sem=recv, device_id=device, device_id_type=MESH
    )


def meet(devices):
    barrier = pltpu.get_barrier_semaphore()
    for device in devices:
        pl.semaphore_signal(barrier, inc=1, device_id=device, device_id_type=MESH)
    pl.semaphore_wait(barrier, len(devices))


def sum_slots(ref):
    total = ref[0]
    for k in range(1, ref.shape[0]):
        total = total + ref[k]
    return total


def merge_stats(blocks, ref):
    parts = [ref[k] for k in range(ref.shape[0])]
    counts = [p[2 * blocks : 2 * blocks + 1] for p in parts]
    count = functools.reduce(jnp.add, counts)
    sums = functools.reduce(jnp.add, [p[0:blocks] for p in parts])
    mean = sums / jnp.maximum(count, 1.0)
    square = jnp.zeros_like(sums)
    for p, n in zip(parts, counts, strict=True):
        gap = p[0:blocks] / jnp.maximum(n, 1.0) - mean
        square = square + (p[blocks : 2 * blocks] + n * gap * gap)
    rest = ref.shape[1] - 2 * blocks - 1
    return jnp.concatenate([sums, square, count, jnp.zeros((rest, LANES), F32)], axis=0)


def stack(row):
    return [row[:, k * LANES : (k + 1) * LANES] for k in range(row.shape[1] // LANES)]


def unstack(value):
    return jnp.concatenate([value[k : k + 1] for k in range(value.shape[0])], axis=1)


def kernel(
    sections, rows, levels, classes,
    feat_ref, wz_ref, wr_ref, wo_ref, whead_ref, count_ref, valid_ref,
    mask_ref, bz_ref, br_ref, bo_ref, gain_ref, shift_ref, bhead_ref, wout_ref, bout_ref, cot_ref,
    gz_out, gr_out, go_out, gfeat_out, ghead_out, logit_out, tiny_out, own_out, aux_out, wfull,
    x_buf, small_buf, par, hs, zs, rs, cs, weight, upper,
    whead, x_hat, logit_buf, dh, d_in, d_reset, gin, vec,
    small_ref, wout_buf, dlog_buf, turn,
    grads, core_buf, total, land,
    h_grads, h_core, h_total, h_land,
    ex_a, ex_a_feat, ex_a_rows, ex_b, ex_b_feat, ex_b_rows,
    ex_c, ex_c_feat, ex_c_mid, ex_c_rows, ex_d, ex_d_feat,
    first_s, first_r, first_l, fy_s, fy_r, a_s, a_r, x_s, x_r, z_s, z_r, b_s, b_r, c_s, c_r,
    own_s, own_r, far_s, far_r, load_w, logit_s, logit_r, gf_s, gf_r, gf_l,
    ef_s, ef_r, er_s, er_r,
    core_s, core_r, rs_s, rs_r, ag_s, ag_r, out_l, hu_s, hu_r, hu_l,
):
    r, f = lax.axis_index("rows"), lax.axis_index("feat")
    weights = (wz_ref, wr_ref, wo_ref)
    units = 3 * sections
    depth = wz_ref.shape[1]
    cuts = cuts_of(levels)
    slots = 3 * cuts
    mine, width = x_buf.shape
    blocks = small_buf.shape[0]
    half = width // 2
    core, far, both = flip(f, 1), flip(f, 2), flip(flip(f, 1), 2)
    others = (core, far, both)
    rx, rz = flip(r, 1), flip(r, 2)
    quarter = depth // 4
    cut_b, cut_c = quarter // 8, quarter // 8 + 7 * quarter // 16
    final = sections - 1
    q = 2 * (r % 2) + (r // 2) % 2
    q_x, q_z, q_d = flip(q, 2), flip(q, 1), flip(flip(q, 1), 2)

    def lanes(index):
        return pl.ds(pl.multiple_of(index * LANES, LANES), LANES)

    def part(start, size):
        return pl.ds(pl.multiple_of(start, 8), size)

    def rows_of(index, start, size):
        return part(index * quarter + start, size)

    meet([(r, peer) for peer in others] + [(lax.rem(r + k, rows), f) for k in range(1, rows)])

    small_ref[...] = jnp.zeros_like(small_ref)
    for k, ref in enumerate((mask_ref, bz_ref, br_ref, bo_ref)):
        small_ref[k * sections : (k + 1) * sections] = ref[...]
    small_ref[4 * sections : 4 * sections + 1] = gain_ref[...]
    small_ref[4 * sections + 1 : 4 * sections + 2] = shift_ref[...]
    own_rows = pl.ds(pl.multiple_of(f * mine, mine), mine)
    firsts, heads = [], []
    for k, peer in enumerate(others):
        chunk = pl.ds(pl.multiple_of(peer * mine, mine), mine)
        firsts += [
            remote(small_ref, small_buf.at[f], first_s.at[k], first_r.at[k], (r, peer)),
            remote(feat_ref.at[chunk], x_buf.at[:, lanes(f)], first_s.at[3 + k], first_r.at[3 + k], (r, peer)),
        ]
        heads.append(remote(whead_ref, whead.at[lanes(f)], first_s.at[6 + k], first_r.at[6 + k], (r, peer)))
    locals_ = [
        pltpu.make_async_copy(small_ref, small_buf.at[f], first_l.at[0]),
        pltpu.make_async_copy(feat_ref.at[own_rows], x_buf.at[:, lanes(f)], first_l.at[1]),
        pltpu.make_async_copy(whead_ref, whead.at[lanes(f)], first_l.at[2]),
    ]

    def y_copy(s, m):
        u, span = 3 * s + m, rows_of(q, 0, quarter)
        return remote(weights[m].at[s, span], wfull.at[s, m, f, span], fy_s.at[u], fy_r.at[u], (r, far))

    def a_copy(s, m, whole=False):
        u, span = 3 * s + m, rows_of(q_d, 0, quarter if whole else cut_b)
        return remote(weights[m].at[s, span], wfull.at[s, m, f, span], a_s.at[u], a_r.at[u], (r, far))

    def own_copy(s, m):
        u = 3 * s + m
        return remote(weights[m].at[s], wfull.at[s, m, f], own_s.at[u], own_r.at[u], (r, core))

    def pass_on(s, m, span, send, recv, device):
        u, ref = 3 * s + m, wfull.at[s, m, far, span]
        return remote(ref, ref, send.at[u], recv.at[u], device)

    def x_copy(s, m):
        return pass_on(s, m, rows_of(q, 0, quarter), x_s, x_r, (rx, f))

    def z_copy(s, m):
        return pass_on(s, m, rows_of(q, 0, quarter), z_s, z_r, (rz, f))

    def b_copy(s, m):
        return pass_on(s, m, rows_of(q_z, cut_b, cut_c - cut_b), b_s, b_r, (rx, f))

    def c_copy(s, m):
        return pass_on(s, m, rows_of(q_x, cut_c, quarter - cut_c), c_s, c_r, (rz, f))

    def far_copy(s, m):
        u, ref = 3 * s + m, wfull.at[s, m, far]
        return remote(ref, ref, far_s.at[u], far_r.at[u], (r, core))

    def w_load(s, m):
        copies = [pltpu.make_async_copy(weights[m].at[s], weight.at[m, :, lanes(f)], load_w.at[m, 0])]
        for k, b in enumerate(others):
            copies.append(
                pltpu.make_async_copy(wfull.at[s, m, b], weight.at[m, :, lanes(b)], load_w.at[m, 1 + k])
            )
        return copies

    def start(copies):
        for copy in copies:
            copy.start()

    def wait(copies):
        for copy in copies:
            copy.wait()

    def send_own(s, whole=False):
        for m in range(3):
            y_copy(s, m).start()
            a_copy(s, m, whole).start()
            own_copy(s, m).start()

    send_own(0)
    start(firsts + locals_)

    @pl.loop(1, final)
    def _(s):
        send_own(s)

    send_own(final, True)
    start(heads)

    def arrange():
        for copy in firsts:
            copy.wait_recv()
        wait(locals_)
        par[...] = jnp.concatenate([small_buf[b] for b in range(blocks)], axis=1)
        logits = par[0:8]
        probs = jnp.exp(logits - jnp.max(logits, axis=1, keepdims=True))
        probs = probs / jnp.sum(probs, axis=1, keepdims=True)
        par[0:sections] = (width * probs)[0:sections]
        hs[0] = x_buf[...]

    def put(value, at_rows):
        for k, piece in enumerate(split(value)):
            upper[k, :, at_rows] = piece

    low_cols, high_cols = slice(0, width), slice(width, 2 * width)

    def product(s, m):
        tiles = []
        for t in range(2):
            w = split(weight[m, :, t * half : (t + 1) * half])
            tiles.append(dot3((upper[0], upper[1]), w, NN))
        return jnp.concatenate(tiles, axis=1) + par[pl.ds(sections * (m + 1) + s, 1), :]

    def gate(s, m):
        if m == 0:
            put(hs[s], low_cols)
            put(x_buf[...] * par[pl.ds(s, 1), :], high_cols)
            zs[s] = jax.nn.sigmoid(product(s, 0))
        elif m == 1:
            rs[s] = jax.nn.sigmoid(product(s, 1))
            put(rs[s] * hs[s], low_cols)
        else:
            cand = jnp.tanh(product(s, 2))
            cs[s] = cand
            hs[s + 1] = hs[s] + zs[s] * (cand - hs[s])

    def at(step, m, back_by):
        u = m - back_by
        return step + u // 3, u % 3

    @pl.loop(0, sections + -(-GATE // 3))
    def _(step):
        for m in range(3):

            @pl.when(step < sections)
            def _():
                y_copy(step, m).wait_recv()
                x_copy(step, m).start()
                z_copy(step, m).start()

            s1, m1 = at(step, m, RELAY)

            @pl.when((s1 >= 0) & (s1 < sections))
            def _():
                x_copy(s1, m1).wait_recv()
                z_copy(s1, m1).wait_recv()

            @pl.when((s1 >= 0) & (s1 < final))
            def _():
                b_copy(s1, m1).start()
                c_copy(s1, m1).start()

            s2, m2 = at(step, m, CORE)

            @pl.when((s2 >= 0) & (s2 < final))
            def _():
                a_copy(s2, m2).wait_recv()
                b_copy(s2, m2).wait_recv()
                c_copy(s2, m2).wait_recv()
                far_copy(s2, m2).start()

            @pl.when(s2 == final)
            def _():
                a_copy(s2, m2, True).wait_recv()
                far_copy(s2, m2).start()

            s3, m3 = at(step, m, LOAD)

            @pl.when((s3 >= 0) & (s3 < sections))
            def _():
                own_copy(s3, m3).wait_recv()
                far_copy(s3, m3).wait_recv()
                start(w_load(s3, m3))

            if m == LOAD % 3:
                pl.when(step == LOAD // 3)(arrange)
            s4, m4 = at(step, m, GATE)

            @pl.when((s4 >= 0) & (s4 < sections))
            def _():
                wait(w_load(s4, m4))
                gate(s4, m4)

    def feat_step(n, src, slots):
        return [
            remote(src, slots.at[f], ef_s.at[n, k], ef_r.at[n, k], (r, peer)) for k, peer in enumerate(others)
        ]

    def rows_step(n, src, slots):
        return [
            remote(src, slots.at[r], er_s.at[n, k - 1], er_r.at[n, k - 1], (lax.rem(r + k, rows), f))
            for k in range(1, rows)
        ]

    unsent = []

    def sum_all(n, value, src, feat_slots, row_slots, merge, meanwhile):
        feat_slots[f] = value
        src[0] = value
        copies = feat_step(n, src.at[0], feat_slots)
        start(copies)
        unsent.extend(copies)
        for copy in copies:
            copy.wait_recv()
        value = merge(feat_slots)
        row_slots[r] = value
        src[1] = value
        copies = rows_step(n, src.at[1], row_slots)
        start(copies)
        unsent.extend(copies)
        done = meanwhile()
        for copy in copies:
            copy.wait_recv()
        return merge(row_slots), done

    for m in (2, 0, 1):
        start(w_load(sections - 1, m))
    here = pl.ds(pl.multiple_of(f * mine, mine), mine)
    place = lax.broadcasted_iota(jnp.int32, (1, mine), 1) + f * mine
    flat = jnp.where(place < count_ref[0], 1.0, 0.0) * valid_ref[:, here].astype(F32)
    column = jnp.transpose(jnp.broadcast_to(flat, (8, mine)))[:, 0:1]
    current = hs[sections]
    count = jnp.sum(column, axis=0, keepdims=True)
    sums = jnp.sum(column * current, axis=0, keepdims=True)
    gap = current - sums / jnp.maximum(count, 1.0)
    square = jnp.sum(column * gap * gap, axis=0, keepdims=True)
    rest = jnp.zeros((ex_a.shape[1] - 2 * blocks - 1, LANES), F32)
    stats = jnp.concatenate(stack(sums) + stack(square) + [jnp.broadcast_to(count, (1, LANES)), rest], axis=0)

    def prepare():
        wout_buf[...] = jnp.zeros_like(wout_buf)
        wout_buf[0:classes] = wout_ref[...]
        dlog_buf[...] = jnp.zeros_like(dlog_buf)
        dlog_buf[0:classes] = cot_ref[:, here] * flat
        turn[...] = jnp.zeros_like(turn)
        turn[0:1, 0:classes] = bout_ref[...]
        b_out = jnp.transpose(turn[...])[0:TALL, 0:1]
        for copy in heads:
            copy.wait_recv()
        d_log = split(dlog_buf[...])
        w_out = split(wout_buf[...])
        return d_log, w_out, dot3(d_log, w_out, TN), b_out

    stats, prepared = sum_all(0, stats, ex_a, ex_a_feat, ex_a_rows, functools.partial(merge_stats, blocks), prepare)
    d_log, w_out, d_hidden, b_out = prepared
    count = stats[2 * blocks : 2 * blocks + 1, 0:1]
    inv_std = lax.rsqrt(unstack(stats[blocks : 2 * blocks]) / count + 1e-05)
    x_hat[...] = (current - unstack(stats[0:blocks]) / count) * inv_std
    gain, shift = par[4 * sections : 4 * sections + 1], par[4 * sections + 1 : 4 * sections + 2]
    normed = split(x_hat[...] * gain + shift)
    w_head = split(whead[...])
    act = dot3(normed, w_head, NN) + bhead_ref[...]
    phi = 0.5 * (1.0 + lax.erf(act * 0.7071067811865476))
    slope = phi + act * (jnp.exp(-0.5 * act * act) * 0.3989422804014327)
    d_act = d_hidden * slope
    d_act2 = split(d_act)
    d_normed = dot3(d_act2, w_head, NT)
    sums = jnp.concatenate(
        stack(jnp.sum(d_normed * x_hat[...], axis=0, keepdims=True))
        + stack(jnp.sum(d_normed, axis=0, keepdims=True)),
        axis=0,
    )
    dh[...] = d_normed
    hid = act.shape[1]
    aux = 4 * sections
    logit_copies = [
        remote(logit_buf.at[f], logit_buf.at[f], logit_s.at[k], logit_r.at[k], (r, peer))
        for k, peer in enumerate(others)
    ]

    def head_rest():
        hidden = split(act * phi)
        logit_buf[f] = (dot3(w_out, hidden, NT) + b_out) * flat
        start(logit_copies)
        vec[...] = jnp.zeros_like(vec)
        vec[aux : aux + TALL, 0:hid] = dot3(d_log, hidden, NN)
        vec[aux + classes : aux + classes + 1, 0:hid] = jnp.sum(d_act, axis=0, keepdims=True)
        ones = split(jnp.ones((8, mine), F32))
        vec[aux + classes + 1 : aux + classes + 2, 0:TALL] = dot3(ones, d_log, NT)[0:1]
        grad = dot3(normed, d_act2, TN)
        for b in range(blocks):
            for t in range(hid // LANES):
                h_grads[b, t * LANES : (t + 1) * LANES] = grad[
                    b * LANES : (b + 1) * LANES, t * LANES : (t + 1) * LANES
                ]
        start(HeadUnit().core_copies())

    outs = (go_out, gz_out, gr_out)
    which = (2, 0, 1)
    peers = [(flip(r, 2**k), f) for k in range(levels)]
    piece = depth // cuts
    held, landed = rings(levels)
    kinds = orders(levels)

    class Unit:
        def __init__(self, step, j, kind="A"):
            m, cut = j // cuts, j % cuts
            span = pl.ds(cut * piece, piece)
            where = (step % 3) * slots + j
            self.depth = piece
            self.grads = grads.at[(3 * step + m) % 2, :, span]
            self.core, self.total, self.land = core_buf.at[j], total.at[step % held, j], land.at[step % landed, j]
            self.out = outs[m].at[sections - 1 - step, span]
            self.core_sems = [(core_s.at[k, j], core_r.at[k, j]) for k in range(2)]
            self.rs_sems = [(rs_s.at[k, step % landed, j], rs_r.at[k, step % landed, j]) for k in range(levels + 2)]
            self.ag_sems = [(ag_s.at[k, where], ag_r.at[k, where]) for k in range(levels)]
            self.out_sem = out_l.at[where]
            self.plan(order_of(kind, levels))

        def plan(self, order):
            self.moves, self.backs = [], []
            base, size, block_list, landing, sem = 0, self.depth, [0, 1], 0, 0
            for step in order:
                move = []
                if step == "y":
                    device, sent, kept, from_blocks, block_list = (r, far), base, base, [1], [0]
                else:
                    size //= 2
                    side = (r // 2**step) % 2
                    device, sent, kept, from_blocks = (
                        peers[step], base + (1 - side) * size, base + side * size, block_list,
                    )
                    self.backs.append((device, part(kept, size)))
                for k, block in enumerate(from_blocks):
                    move.append(
                        (device, block, part(sent, size), block_list[k], part(kept, size),
                         pl.ds(landing, size), self.rs_sems[sem])
                    )
                    landing += size
                    sem += 1
                self.moves.append(move)
                base = kept
            self.backs.reverse()

        def core_copies(self):
            return [
                remote(self.grads.at[b], self.core.at[k], *self.core_sems[k], (r, core))
                for k, b in enumerate((core, both))
            ]

        def rs_copies(self, i):
            return [
                remote(self.total.at[block, sent], self.land.at[landing], *sems, device)
                for device, block, sent, _, _, landing, sems in self.moves[i]
            ]

        def add(self, i):
            for _, _, _, block, kept, landing, _ in self.moves[i]:
                self.total[block, kept] += self.land[landing]

        def ag_copy(self, i):
            device, kept = self.backs[i]
            dst = self.out.at[kept]
            return remote(self.total.at[0, kept] if i == 0 else dst, dst, *self.ag_sems[i], device)

        def out_local(self):
            kept = self.backs[0][1]
            return pltpu.make_async_copy(self.total.at[0, kept], self.out.at[kept], self.out_sem)

    class HeadUnit(Unit):
        def __init__(self):
            self.depth = h_grads.shape[1]
            self.grads, self.core, self.total, self.land, self.out = h_grads, h_core, h_total, h_land, ghead_out
            sems = [(hu_s.at[k], hu_r.at[k]) for k in range(2 * levels + 4)]
            self.core_sems, self.rs_sems, self.ag_sems = sems[:2], sems[2 : levels + 4], sems[levels + 4 :]
            self.out_sem = hu_l.at[0]
            self.plan(order_of("A", levels))

    def stage_core(unit):
        wait(unit.core_copies())
        unit.total[1] = unit.grads[far] + unit.core[1]
        unit.total[0] = unit.grads[f] + unit.core[0]
        start(unit.rs_copies(0))

    def stage_sum(i, unit):
        wait(unit.rs_copies(i))
        unit.add(i)
        if i < levels:
            start(unit.rs_copies(i + 1))
        else:
            unit.ag_copy(0).start()
            unit.out_local().start()

    def stage_out(i, unit):
        if i == 0:
            unit.out_local().wait()
        unit.ag_copy(i).wait()
        if i + 1 < levels:
            unit.ag_copy(i + 1).start()

    stages = [stage_core]
    stages += [functools.partial(stage_sum, i) for i in range(levels + 1)]
    stages += [functools.partial(stage_out, i) for i in range(levels)]

    def outer(m, u, right):
        for t in range(2):
            tile = split(right[:, t * half : (t + 1) * half])
            tile = dot3((upper[0], upper[1]), tile, TN)
            for b in range(half // LANES):
                grads[u % 2, t * (half // LANES) + b] = tile[:, b * LANES : (b + 1) * LANES]

    def back(m, left, t):
        return dot3(left, split(weight[which[m], t * half : (t + 1) * half, :]), NT)

    def compute(step, m, ready):
        s = sections - 1 - step
        u = 3 * step + m
        wait(w_load(s, which[m]))
        h = hs[s]
        if m == 0:
            z, reset, c = zs[s], rs[s], cs[s]
            put(reset * h, low_cols)
            put(x_buf[...] * par[pl.ds(s, 1), :], high_cols)
            d_out = dh[...] * z * (1.0 - c * c)
            vec[pl.ds(2 * sections + s, 1), :] = jnp.sum(d_out, axis=0, keepdims=True)
            outer(m, u, d_out)
            ready()
            left = split(d_out)
            for t in range(4):
                d_in[:, t * half : (t + 1) * half] = back(m, left, t)
            d_reset[...] = d_in[:, 0:width] * h * reset * (1.0 - reset)
        elif m == 1:
            z, reset, c = zs[s], rs[s], cs[s]
            put(h, low_cols)
            d_up = dh[...] * (c - h) * z * (1.0 - z)
            vec[pl.ds(s, 1), :] = jnp.sum(d_up, axis=0, keepdims=True)
            outer(m, u, d_up)
            ready()
            dh[...] = dh[...] * (1.0 - z) + d_in[:, 0:width] * reset
            left = split(d_up)
            for t in range(4):
                cols = slice(t % 2 * half, (t % 2 + 1) * half)
                if t < 2:
                    dh[:, cols] += back(m, left, t)
                else:
                    d_in[:, t * half : (t + 1) * half] += back(m, left, t)
        else:
            d_r = d_reset[...]
            vec[pl.ds(sections + s, 1), :] = jnp.sum(d_r, axis=0, keepdims=True)
            outer(m, u, d_r)
            ready()
            left = split(d_r)
            for t in range(4):
                cols = slice(t % 2 * half, (t % 2 + 1) * half)
                if t < 2:
                    dh[:, cols] += back(m, left, t)
                else:
                    d_xs = d_in[:, t * half : (t + 1) * half] + back(m, left, t)
                    gin[:, cols] += d_xs * par[pl.ds(s, 1), cols]
                    vec[pl.ds(3 * sections + s, 1), cols] = jnp.sum(d_xs * x_buf[:, cols], axis=0, keepdims=True)

        @pl.when(step + 1 < sections)
        def _():
            start(w_load(s - 1, which[m]))

    gf_copies = [
        remote(gin.at[:, lanes(peer)], gfeat_out.at[own_rows], gf_s.at[k], gf_r.at[k], (r, peer))
        for k, peer in enumerate(others)
    ]
    gf_local = pltpu.make_async_copy(gin.at[:, lanes(f)], gfeat_out.at[own_rows], gf_l.at[0])
    vec_feat = [
        remote(ex_c.at[peer], ex_c_feat.at[f], ef_s.at[2, k], ef_r.at[2, k], (r, peer)) for k, peer in enumerate(others)
    ]
    vec_rows = rows_step(2, ex_c_mid, ex_c_rows)
    vec_last = feat_step(3, ex_d, ex_d_feat)
    spread = hid // LANES

    sums, _ = sum_all(1, sums, ex_b, ex_b_feat, ex_b_rows, sum_slots, head_rest)
    g_gain, g_shift = unstack(sums[0:blocks]), unstack(sums[blocks:])
    dh[...] = inv_std * (dh[...] * gain - column / count * gain * (g_shift + x_hat[...] * g_gain))
    tiny_out[...] = sums
    gin[...] = jnp.zeros_like(gin)

    def before(step, j, back_by):
        u = j - back_by
        return step + u // slots, u % slots

    delays = schedule(levels)

    @pl.loop(0, sections + -(-delays[-1] // slots))
    def _(step):
        for j in range(slots):

            @pl.when(step < sections)
            def _():
                def ready():
                    start(Unit(step, j).core_copies())

                if j % cuts == 0:
                    compute(step, j // cuts, ready)
                else:
                    ready()

            for delay, stage in zip(delays, stages, strict=True):
                s1, j1 = before(step, j, delay)
                if j1 == slots - 1:

                    @pl.when(s1 == -1)
                    def _():
                        stage(HeadUnit())

                groups = (s1 == 0, (s1 > 0) & (s1 < sections - 1), s1 == sections - 1)
                for kind in sorted({row[j1] for row in kinds}):
                    active = [g for g, row in zip(groups, kinds, strict=True) if row[j1] == kind]

                    @pl.when(functools.reduce(jnp.logical_or, active))
                    def _():
                        stage(Unit(s1, j1, kind))

            if j == 0:

                @pl.when(step == sections)
                def _():
                    for b in range(blocks):
                        ex_c[b, 0:aux] = vec[0:aux, b * LANES : (b + 1) * LANES]
                        ex_c[b, aux : aux + 8] = vec[
                            aux + 8 * (b // spread) : aux + 8 * (b // spread + 1),
                            LANES * (b % spread) : LANES * (b % spread + 1),
                        ]
                    ex_c_feat[f] = ex_c[f]
                    start(vec_feat)
                    gin[...] += dh[...]
                    start(gf_copies + [gf_local])

            if j == 2:

                @pl.when(step == sections)
                def _():
                    wait(vec_feat)
                    ex_c_mid[...] = sum_slots(ex_c_feat)
                    ex_c_rows[r] = ex_c_mid[...]
                    start(vec_rows)

            if j == 5:

                @pl.when(step == sections)
                def _():
                    wait(vec_rows)
                    sums = sum_slots(ex_c_rows)
                    own_out[...] = sums[0:aux]
                    scale = par[0:sections, lanes(f)]
                    inner = jnp.sum(scale * sums[3 * sections : aux], axis=1, keepdims=True) / width
                    ex_d[...] = jnp.zeros_like(ex_d)
                    ex_d[0:sections] = jnp.broadcast_to(inner, (sections, LANES))
                    ex_d[8:16] = sums[aux : aux + 8]
                    ex_d_feat[f] = ex_d[...]
                    start(vec_last)

    wait(vec_last)
    inner = sum_slots(ex_d_feat)[0:sections]
    own_out[3 * sections : aux] = par[0:sections, lanes(f)] * (own_out[3 * sections : aux] - inner)
    for b in range(blocks):
        aux_out[8 * (b // spread) : 8 * (b // spread + 1), LANES * (b % spread) : LANES * (b % spread + 1)] = (
            ex_d_feat[b, 8:16]
        )
    wait(gf_copies + [gf_local])
    wait(logit_copies)
    for b in range(blocks):
        logit_out[:, b * mine : (b + 1) * mine] = logit_buf[b]

    @pl.loop(0, sections)
    def _(s):
        for m in range(3):
            for copy in (y_copy, own_copy, x_copy, z_copy, far_copy):
                copy(s, m).wait_send()

    @pl.loop(0, final)
    def _(s):
        for m in range(3):
            for copy in (a_copy, b_copy, c_copy):
                copy(s, m).wait_send()

    for m in range(3):
        a_copy(final, m, True).wait_send()

    for copy in firsts + heads + unsent:
        copy.wait_send()


def finish_kernel(
    sections, classes,
    gz_ref, gr_ref, go_ref, gfeat_ref, ghead_ref, logit_ref, tiny_ref, own_ref, aux_ref,
    logit_out, gfeat_out, gmask_out, gz_out, gr_out, go_out, bz_out, br_out, bo_out,
    gain_out, shift_out, ghead_out, bhead_out, wout_out, bout_out,
    store,
):
    f = lax.axis_index("feat")
    pairs = [(gfeat_ref, gfeat_out)] + [
        (src.at[s], dst.at[s])
        for s in range(sections)
        for src, dst in ((gz_ref, gz_out), (gr_ref, gr_out), (go_ref, go_out))
    ]
    stores = [pltpu.make_async_copy(src, dst, store.at[k]) for k, (src, dst) in enumerate(pairs)]
    for copy in stores:
        copy.start()
    block = gfeat_ref.shape[1]
    hidden = bhead_out.shape[1]
    logit_out[...] = logit_ref[0:classes]
    for k, out in enumerate((bz_out, br_out, bo_out, gmask_out)):
        out[...] = own_ref[k * sections : (k + 1) * sections]
    gain_out[...] = tiny_ref[pl.ds(f, 1)]
    shift_out[...] = tiny_ref[pl.ds(tiny_ref.shape[0] // 2 + f, 1)]
    for t in range(hidden // block):
        ghead_out[:, t * block : (t + 1) * block] = ghead_ref[t * block : (t + 1) * block]
    wout_out[...] = aux_ref[0:classes]
    bhead_out[...] = aux_ref[classes : classes + 1]
    bout_out[...] = aux_ref[classes + 1 : classes + 2, 0:classes]
    for copy in stores:
        copy.wait()


def layer(
    rows, groups, features, w_update, w_reset, w_candidate, w_head, counts, validity, mask_logits, b_update, b_reset,
    b_candidate, norm_gain, norm_shift, b_head, w_out, b_out, cotangent,
):
    sections, depth, block = w_update.shape
    width, mine = groups * block, features.shape[0] // groups
    hidden = w_head.shape[1]
    classes = w_out.shape[0]
    units = 3 * sections
    levels = rows.bit_length() - 1
    head_depth = max(hidden, 8 * rows)
    cuts = cuts_of(levels)
    slots = 3 * cuts
    piece = depth // cuts
    held, landed = rings(levels)
    long = 4 * sections + TALL
    sds = jax.ShapeDtypeStruct
    dma = pltpu.SemaphoreType.DMA
    any_, vmem = pl.BlockSpec(memory_space=pl.ANY), pl.BlockSpec(memory_space=pltpu.VMEM)
    grad = sds((sections, depth, block), F32)
    held_grad = pltpu.VMEM((sections, depth, block), F32)

    def buf(*shape):
        return pltpu.VMEM(shape, F32)

    made = pl.pallas_call(
        functools.partial(kernel, sections, rows, levels, classes),
        out_shape=[
            held_grad, held_grad, held_grad,
            pltpu.VMEM(features.shape, F32),
            pltpu.VMEM((head_depth, block), F32),
            pltpu.VMEM((TALL, groups * mine), F32),
            pltpu.VMEM((2 * groups, block), F32),
            pltpu.VMEM((4 * sections, block), F32),
            pltpu.VMEM((TALL, hidden), F32),
            sds((sections, 3, groups, depth, block), F32),
        ],
        in_specs=[any_] * 5 + [pl.BlockSpec(memory_space=pltpu.SMEM)] + [vmem] * 11,
        out_specs=[vmem] * 9 + [any_],
        scratch_shapes=[
            buf(mine, width), buf(groups, PAR, block), buf(PAR, width), buf(sections + 1, mine, width),
            buf(sections, mine, width), buf(sections, mine, width), buf(sections, mine, width),
            buf(3, depth, width), pltpu.VMEM((2, mine, depth), BF16),
            buf(width, hidden), buf(mine, width), buf(groups, TALL, mine), buf(mine, width),
            buf(mine, depth), buf(mine, width), buf(mine, width), buf(long, width),
            buf(PAR, block), buf(TALL, hidden), buf(TALL, mine), buf(8, LANES),
            buf(2, groups, depth, block), buf(slots, 2, piece, block), buf(held, slots, 2, piece, block),
            buf(landed, slots, 2 * piece, block),
            buf(groups, head_depth, block), buf(2, head_depth, block), buf(2, head_depth, block),
            buf(2 * head_depth, block),
            buf(2, 16, LANES), buf(groups, 16, LANES), buf(rows, 16, LANES),
            buf(2, 2 * groups, LANES), buf(groups, 2 * groups, LANES), buf(rows, 2 * groups, LANES),
            buf(groups, 4 * sections + 8, block), buf(groups, 4 * sections + 8, block), buf(4 * sections + 8, block),
            buf(rows, 4 * sections + 8, block), buf(16, block), buf(groups, 16, block),
            dma((9,)), dma((9,)), dma((3,)),
        ] + [dma((units,))] * 16 + [
            dma((3, groups)), dma((3,)), dma((3,)), dma((3,)), dma((3,)), dma((1,)),
            dma((4, 3)), dma((4, 3)), dma((3, rows - 1)), dma((3, rows - 1)),
            dma((2, slots)), dma((2, slots)), dma((levels + 2, landed, slots)), dma((levels + 2, landed, slots)),
            dma((levels, 3 * slots)), dma((levels, 3 * slots)), dma((3 * slots,)),
            dma((2 * levels + 4,)), dma((2 * levels + 4,)), dma((1,)),
        ],
        compiler_params=pltpu.CompilerParams(
            collective_id=0, has_side_effects=True, vmem_limit_bytes=52 * 2**20
        ),
    )(
        features, w_update, w_reset, w_candidate, w_head, counts, validity[None], mask_logits, b_update, b_reset,
        b_candidate, norm_gain[None], norm_shift[None], b_head[None], w_out, b_out[None], cotangent,
    )
    row = sds((1, block), F32)
    bias = sds((sections, block), F32)
    return pl.pallas_call(
        functools.partial(finish_kernel, sections, classes),
        out_shape=[
            sds((classes, groups * mine), F32), sds(features.shape, F32), bias, grad, grad, grad, bias, bias, bias,
            row, row, sds((block, hidden), F32), sds((1, hidden), F32), sds((classes, hidden), F32),
            sds((1, classes), F32),
        ],
        in_specs=[vmem] * 3 + [vmem] + [vmem] * 5,
        out_specs=[vmem, any_, vmem, any_, any_, any_] + [vmem] * 9,
        scratch_shapes=[dma((units + 1,))],
        compiler_params=pltpu.CompilerParams(vmem_limit_bytes=16 * 2**20),
    )(*made[:9])


def local(
    rows, groups, features, counts, validity, mask_logits, w_update, w_reset, w_candidate, b_update, b_reset,
    b_candidate, norm_gain, norm_shift, w_head, b_head, w_out, b_out, cotangent,
):
    out = layer(
        rows, groups, features, w_update, w_reset, w_candidate, w_head, counts, validity, mask_logits, b_update,
        b_reset, b_candidate, norm_gain, norm_shift, b_head, w_out.T, b_out, cotangent.T,
    )
    logits, g_feat, g_mask, gz, gr, go, bz, br, bo, gain, shift, g_head, g_b_head, g_w_out, g_b_out = out
    return (
        logits.T, g_feat, g_mask, gz, gr, go, bz, br, bo, gain[0], shift[0], g_head, g_b_head[0], g_w_out.T,
        g_b_out[0],
    )


def solution(mesh):
    rows, groups = mesh.shape["rows"], mesh.shape["feat"]
    split_cols, by_feat = P(None, None, "feat"), P("feat")
    return jax.shard_map(
        functools.partial(local, rows, groups),
        mesh=mesh,
        in_specs=(
            P("rows", "feat"), P("rows"), P("rows"), P(None, "feat"), split_cols, split_cols, split_cols,
            P(None, "feat"), P(None, "feat"), P(None, "feat"), by_feat, by_feat, P("feat", None),
            P(), P(), P(), P("rows", None),
        ),
        out_specs=(
            P("rows", None), P("rows", "feat"), P(None, "feat"), split_cols, split_cols, split_cols,
            P(None, "feat"), P(None, "feat"), P(None, "feat"), by_feat, by_feat, P("feat", None),
            P(), P(), P(),
        ),
        check_vma=False,
    )
```

```python
import functools

import jax
import jax.numpy as jnp
from jax import lax
from jax.experimental import pallas as pl
from jax.experimental.pallas import tpu as pltpu
from jax.sharding import PartitionSpec as P

MESH = pl.DeviceIdType.MESH
F32, BF16 = jnp.float32, jnp.bfloat16
LANES = 128
PAR = 32
TALL = 16
RELAY, CORE, LOAD, GATE = 1, 2, 3, 4


def cuts_of(levels):
    return 4 if levels < 6 else 2


def orders(levels):
    if levels == 3:
        return "EAXAEAXEEAXX", "EXBABXAAAAAA", "BAAABABBXBXB"
    return ("A" * (3 * cuts_of(levels) - 1) + "E",) * 3


def order_of(kind, levels):
    start = {"A": ["y", 0, 1], "E": [1, "y", 0], "B": ["y", 1, 0], "X": [0, "y", 1]}[kind]
    return start + list(range(2, levels))


def schedule(levels):
    if levels == 3:
        return [3, 7, 11, 14, 16, 18, 21, 28]
    return list(range(1, 2 * levels + 3))


def rings(levels):
    return -(-(schedule(levels)[levels + 2] + 1) // (3 * cuts_of(levels))), 2


def flip(index, stride):
    return index + stride - 2 * stride * ((index // stride) % 2)


def split(value):
    high = value.astype(BF16)
    return high, (value - high.astype(F32)).astype(BF16)


def dot3(left, right, dims):
    def one(a, b):
        return lax.dot_general(a, b, (dims, ((), ())), preferred_element_type=F32)

    return one(left[0], right[1]) + one(left[1], right[0]) + one(left[0], right[0])


NN, NT, TN = ((1,), (0,)), ((1,), (1,)), ((0,), (0,))


def remote(src, dst, send, recv, device):
    return pltpu.make_async_remote_copy(
        src_ref=src, dst_ref=dst, send_sem=send, recv_sem=recv, device_id=device, device_id_type=MESH
    )


def meet(devices):
    barrier = pltpu.get_barrier_semaphore()
    for device in devices:
        pl.semaphore_signal(barrier, inc=1, device_id=device, device_id_type=MESH)
    pl.semaphore_wait(barrier, len(devices))


def sum_slots(ref):
    total = ref[0]
    for k in range(1, ref.shape[0]):
        total = total + ref[k]
    return total


def merge_stats(blocks, ref):
    parts = [ref[k] for k in range(ref.shape[0])]
    counts = [p[2 * blocks : 2 * blocks + 1] for p in parts]
    count = functools.reduce(jnp.add, counts)
    sums = functools.reduce(jnp.add, [p[0:blocks] for p in parts])
    mean = sums / jnp.maximum(count, 1.0)
    square = jnp.zeros_like(sums)
    for p, n in zip(parts, counts, strict=True):
        gap = p[0:blocks] / jnp.maximum(n, 1.0) - mean
        square = square + (p[blocks : 2 * blocks] + n * gap * gap)
    rest = ref.shape[1] - 2 * blocks - 1
    return jnp.concatenate([sums, square, count, jnp.zeros((rest, LANES), F32)], axis=0)


def stack(row):
    return [row[:, k * LANES : (k + 1) * LANES] for k in range(row.shape[1] // LANES)]


def unstack(value):
    return jnp.concatenate([value[k : k + 1] for k in range(value.shape[0])], axis=1)


def kernel(
    sections, rows, levels, classes,
    feat_ref, wz_ref, wr_ref, wo_ref, whead_ref, count_ref, valid_ref,
    mask_ref, bz_ref, br_ref, bo_ref, gain_ref, shift_ref, bhead_ref, wout_ref, bout_ref, cot_ref,
    gz_out, gr_out, go_out, gfeat_out, ghead_out, logit_out, tiny_out, own_out, aux_out, wfull,
    x_buf, small_buf, par, hs, zs, rs, cs, weight, upper,
    whead, x_hat, logit_buf, dh, d_in, d_reset, gin, vec,
    small_ref, wout_buf, dlog_buf, turn,
    grads, core_buf, total, land,
    h_grads, h_core, h_total, h_land,
    ex_a, ex_a_feat, ex_a_rows, ex_b, ex_b_feat, ex_b_rows,
    ex_c, ex_c_feat, ex_c_mid, ex_c_rows, ex_d, ex_d_feat,
    first_s, first_r, first_l, fy_s, fy_r, a_s, a_r, x_s, x_r, z_s, z_r, b_s, b_r, c_s, c_r,
    own_s, own_r, far_s, far_r, load_w, logit_s, logit_r, gf_s, gf_r, gf_l,
    ef_s, ef_r, er_s, er_r,
    core_s, core_r, rs_s, rs_r, ag_s, ag_r, out_l, hu_s, hu_r, hu_l,
):
    r, f = lax.axis_index("rows"), lax.axis_index("feat")
    weights = (wz_ref, wr_ref, wo_ref)
    units = 3 * sections
    depth = wz_ref.shape[1]
    cuts = cuts_of(levels)
    slots = 3 * cuts
    mine, width = x_buf.shape
    blocks = small_buf.shape[0]
    half = width // 2
    core, far, both = flip(f, 1), flip(f, 2), flip(flip(f, 1), 2)
    others = (core, far, both)
    rx, rz = flip(r, 1), flip(r, 2)
    quarter = depth // 4
    cut_b, cut_c = quarter // 8, quarter // 8 + 7 * quarter // 16
    final = sections - 1
    q = 2 * (r % 2) + (r // 2) % 2
    q_x, q_z, q_d = flip(q, 2), flip(q, 1), flip(flip(q, 1), 2)

    def lanes(index):
        return pl.ds(pl.multiple_of(index * LANES, LANES), LANES)

    def part(start, size):
        return pl.ds(pl.multiple_of(start, 8), size)

    def rows_of(index, start, size):
        return part(index * quarter + start, size)

    meet([(r, peer) for peer in others] + [(lax.rem(r + k, rows), f) for k in range(1, rows)])

    small_ref[...] = jnp.zeros_like(small_ref)
    for k, ref in enumerate((mask_ref, bz_ref, br_ref, bo_ref)):
        small_ref[k * sections : (k + 1) * sections] = ref[...]
    small_ref[4 * sections : 4 * sections + 1] = gain_ref[...]
    small_ref[4 * sections + 1 : 4 * sections + 2] = shift_ref[...]
    own_rows = pl.ds(pl.multiple_of(f * mine, mine), mine)
    firsts, heads = [], []
    for k, peer in enumerate(others):
        chunk = pl.ds(pl.multiple_of(peer * mine, mine), mine)
        firsts += [
            remote(small_ref, small_buf.at[f], first_s.at[k], first_r.at[k], (r, peer)),
            remote(feat_ref.at[chunk], x_buf.at[:, lanes(f)], first_s.at[3 + k], first_r.at[3 + k], (r, peer)),
        ]
        heads.append(remote(whead_ref, whead.at[lanes(f)], first_s.at[6 + k], first_r.at[6 + k], (r, peer)))
    locals_ = [
        pltpu.make_async_copy(small_ref, small_buf.at[f], first_l.at[0]),
        pltpu.make_async_copy(feat_ref.at[own_rows], x_buf.at[:, lanes(f)], first_l.at[1]),
        pltpu.make_async_copy(whead_ref, whead.at[lanes(f)], first_l.at[2]),
    ]

    def y_copy(s, m):
        u, span = 3 * s + m, rows_of(q, 0, quarter)
        return remote(weights[m].at[s, span], wfull.at[s, m, f, span], fy_s.at[u], fy_r.at[u], (r, far))

    def a_copy(s, m, whole=False):
        u, span = 3 * s + m, rows_of(q_d, 0, quarter if whole else cut_b)
        return remote(weights[m].at[s, span], wfull.at[s, m, f, span], a_s.at[u], a_r.at[u], (r, far))

    def own_copy(s, m):
        u = 3 * s + m
        return remote(weights[m].at[s], wfull.at[s, m, f], own_s.at[u], own_r.at[u], (r, core))

    def pass_on(s, m, span, send, recv, device):
        u, ref = 3 * s + m, wfull.at[s, m, far, span]
        return remote(ref, ref, send.at[u], recv.at[u], device)

    def x_copy(s, m):
        return pass_on(s, m, rows_of(q, 0, quarter), x_s, x_r, (rx, f))

    def z_copy(s, m):
        return pass_on(s, m, rows_of(q, 0, quarter), z_s, z_r, (rz, f))

    def b_copy(s, m):
        return pass_on(s, m, rows_of(q_z, cut_b, cut_c - cut_b), b_s, b_r, (rx, f))

    def c_copy(s, m):
        return pass_on(s, m, rows_of(q_x, cut_c, quarter - cut_c), c_s, c_r, (rz, f))

    def far_copy(s, m):
        u, ref = 3 * s + m, wfull.at[s, m, far]
        return remote(ref, ref, far_s.at[u], far_r.at[u], (r, core))

    def w_load(s, m):
        copies = [pltpu.make_async_copy(weights[m].at[s], weight.at[m, :, lanes(f)], load_w.at[m, 0])]
        for k, b in enumerate(others):
            copies.append(
                pltpu.make_async_copy(wfull.at[s, m, b], weight.at[m, :, lanes(b)], load_w.at[m, 1 + k])
            )
        return copies

    def start(copies):
        for copy in copies:
            copy.start()

    def wait(copies):
        for copy in copies:
            copy.wait()

    def send_own(s, whole=False):
        for m in range(3):
            y_copy(s, m).start()
            a_copy(s, m, whole).start()
            own_copy(s, m).start()

    send_own(0)
    start(firsts + locals_)

    @pl.loop(1, final)
    def _(s):
        send_own(s)

    send_own(final, True)
    start(heads)

    def arrange():
        for copy in firsts:
            copy.wait_recv()
        wait(locals_)
        par[...] = jnp.concatenate([small_buf[b] for b in range(blocks)], axis=1)
        logits = par[0:8]
        probs = jnp.exp(logits - jnp.max(logits, axis=1, keepdims=True))
        probs = probs / jnp.sum(probs, axis=1, keepdims=True)
        par[0:sections] = (width * probs)[0:sections]
        hs[0] = x_buf[...]

    def put(value, at_rows):
        for k, piece in enumerate(split(value)):
            upper[k, :, at_rows] = piece

    low_cols, high_cols = slice(0, width), slice(width, 2 * width)

    def product(s, m):
        tiles = []
        for t in range(2):
            w = split(weight[m, :, t * half : (t + 1) * half])
            tiles.append(dot3((upper[0], upper[1]), w, NN))
        return jnp.concatenate(tiles, axis=1) + par[pl.ds(sections * (m + 1) + s, 1), :]

    def gate(s, m):
        if m == 0:
            put(hs[s], low_cols)
            put(x_buf[...] * par[pl.ds(s, 1), :], high_cols)
            zs[s] = jax.nn.sigmoid(product(s, 0))
        elif m == 1:
            rs[s] = jax.nn.sigmoid(product(s, 1))
            put(rs[s] * hs[s], low_cols)
        else:
            cand = jnp.tanh(product(s, 2))
            cs[s] = cand
            hs[s + 1] = hs[s] + zs[s] * (cand - hs[s])

    def at(step, m, back_by):
        u = m - back_by
        return step + u // 3, u % 3

    @pl.loop(0, sections + -(-GATE // 3))
    def _(step):
        for m in range(3):

            @pl.when(step < sections)
            def _():
                y_copy(step, m).wait_recv()
                x_copy(step, m).start()
                z_copy(step, m).start()

            s1, m1 = at(step, m, RELAY)

            @pl.when((s1 >= 0) & (s1 < sections))
            def _():
                x_copy(s1, m1).wait_recv()
                z_copy(s1, m1).wait_recv()

            @pl.when((s1 >= 0) & (s1 < final))
            def _():
                b_copy(s1, m1).start()
                c_copy(s1, m1).start()

            s2, m2 = at(step, m, CORE)

            @pl.when((s2 >= 0) & (s2 < final))
            def _():
                a_copy(s2, m2).wait_recv()
                b_copy(s2, m2).wait_recv()
                c_copy(s2, m2).wait_recv()
                far_copy(s2, m2).start()

            @pl.when(s2 == final)
            def _():
                a_copy(s2, m2, True).wait_recv()
                far_copy(s2, m2).start()

            s3, m3 = at(step, m, LOAD)

            @pl.when((s3 >= 0) & (s3 < sections))
            def _():
                own_copy(s3, m3).wait_recv()
                far_copy(s3, m3).wait_recv()
                start(w_load(s3, m3))

            if m == LOAD % 3:
                pl.when(step == LOAD // 3)(arrange)
            s4, m4 = at(step, m, GATE)

            @pl.when((s4 >= 0) & (s4 < sections))
            def _():
                wait(w_load(s4, m4))
                gate(s4, m4)

    def feat_step(n, src, slots):
        return [
            remote(src, slots.at[f], ef_s.at[n, k], ef_r.at[n, k], (r, peer)) for k, peer in enumerate(others)
        ]

    def rows_step(n, src, slots):
        return [
            remote(src, slots.at[r], er_s.at[n, k - 1], er_r.at[n, k - 1], (lax.rem(r + k, rows), f))
            for k in range(1, rows)
        ]

    unsent = []

    def sum_all(n, value, src, feat_slots, row_slots, merge, meanwhile):
        feat_slots[f] = value
        src[0] = value
        copies = feat_step(n, src.at[0], feat_slots)
        start(copies)
        unsent.extend(copies)
        for copy in copies:
            copy.wait_recv()
        value = merge(feat_slots)
        row_slots[r] = value
        src[1] = value
        copies = rows_step(n, src.at[1], row_slots)
        start(copies)
        unsent.extend(copies)
        done = meanwhile()
        for copy in copies:
            copy.wait_recv()
        return merge(row_slots), done

    for m in (2, 0, 1):
        start(w_load(sections - 1, m))
    here = pl.ds(pl.multiple_of(f * mine, mine), mine)
    place = lax.broadcasted_iota(jnp.int32, (1, mine), 1) + f * mine
    flat = jnp.where(place < count_ref[0], 1.0, 0.0) * valid_ref[:, here].astype(F32)
    column = jnp.transpose(jnp.broadcast_to(flat, (8, mine)))[:, 0:1]
    current = hs[sections]
    count = jnp.sum(column, axis=0, keepdims=True)
    sums = jnp.sum(column * current, axis=0, keepdims=True)
    gap = current - sums / jnp.maximum(count, 1.0)
    square = jnp.sum(column * gap * gap, axis=0, keepdims=True)
    rest = jnp.zeros((ex_a.shape[1] - 2 * blocks - 1, LANES), F32)
    stats = jnp.concatenate(stack(sums) + stack(square) + [jnp.broadcast_to(count, (1, LANES)), rest], axis=0)

    def prepare():
        wout_buf[...] = jnp.zeros_like(wout_buf)
        wout_buf[0:classes] = wout_ref[...]
        dlog_buf[...] = jnp.zeros_like(dlog_buf)
        dlog_buf[0:classes] = cot_ref[:, here] * flat
        turn[...] = jnp.zeros_like(turn)
        turn[0:1, 0:classes] = bout_ref[...]
        b_out = jnp.transpose(turn[...])[0:TALL, 0:1]
        for copy in heads:
            copy.wait_recv()
        d_log = split(dlog_buf[...])
        w_out = split(wout_buf[...])
        return d_log, w_out, dot3(d_log, w_out, TN), b_out

    stats, prepared = sum_all(0, stats, ex_a, ex_a_feat, ex_a_rows, functools.partial(merge_stats, blocks), prepare)
    d_log, w_out, d_hidden, b_out = prepared
    count = stats[2 * blocks : 2 * blocks + 1, 0:1]
    inv_std = lax.rsqrt(unstack(stats[blocks : 2 * blocks]) / count + 1e-05)
    x_hat[...] = (current - unstack(stats[0:blocks]) / count) * inv_std
    gain, shift = par[4 * sections : 4 * sections + 1], par[4 * sections + 1 : 4 * sections + 2]
    normed = split(x_hat[...] * gain + shift)
    w_head = split(whead[...])
    act = dot3(normed, w_head, NN) + bhead_ref[...]
    phi = 0.5 * (1.0 + lax.erf(act * 0.7071067811865476))
    slope = phi + act * (jnp.exp(-0.5 * act * act) * 0.3989422804014327)
    d_act = d_hidden * slope
    d_act2 = split(d_act)
    d_normed = dot3(d_act2, w_head, NT)
    sums = jnp.concatenate(
        stack(jnp.sum(d_normed * x_hat[...], axis=0, keepdims=True))
        + stack(jnp.sum(d_normed, axis=0, keepdims=True)),
        axis=0,
    )
    dh[...] = d_normed
    hid = act.shape[1]
    aux = 4 * sections
    logit_copies = [
        remote(logit_buf.at[f], logit_buf.at[f], logit_s.at[k], logit_r.at[k], (r, peer))
        for k, peer in enumerate(others)
    ]

    def head_rest():
        hidden = split(act * phi)
        logit_buf[f] = (dot3(w_out, hidden, NT) + b_out) * flat
        start(logit_copies)
        vec[...] = jnp.zeros_like(vec)
        vec[aux : aux + TALL, 0:hid] = dot3(d_log, hidden, NN)
        vec[aux + classes : aux + classes + 1, 0:hid] = jnp.sum(d_act, axis=0, keepdims=True)
        ones = split(jnp.ones((8, mine), F32))
        vec[aux + classes + 1 : aux + classes + 2, 0:TALL] = dot3(ones, d_log, NT)[0:1]
        grad = dot3(normed, d_act2, TN)
        for b in range(blocks):
            for t in range(hid // LANES):
                h_grads[b, t * LANES : (t + 1) * LANES] = grad[
                    b * LANES : (b + 1) * LANES, t * LANES : (t + 1) * LANES
                ]
        start(HeadUnit().core_copies())

    outs = (go_out, gz_out, gr_out)
    which = (2, 0, 1)
    peers = [(flip(r, 2**k), f) for k in range(levels)]
    piece = depth // cuts
    held, landed = rings(levels)
    kinds = orders(levels)

    class Unit:
        def __init__(self, step, j, kind="A"):
            m, cut = j // cuts, j % cuts
            span = pl.ds(cut * piece, piece)
            where = (step % 3) * slots + j
            self.depth = piece
            self.grads = grads.at[(3 * step + m) % 2, :, span]
            self.core, self.total, self.land = core_buf.at[j], total.at[step % held, j], land.at[step % landed, j]
            self.out = outs[m].at[sections - 1 - step, span]
            self.core_sems = [(core_s.at[k, j], core_r.at[k, j]) for k in range(2)]
            self.rs_sems = [(rs_s.at[k, step % landed, j], rs_r.at[k, step % landed, j]) for k in range(levels + 2)]
            self.ag_sems = [(ag_s.at[k, where], ag_r.at[k, where]) for k in range(levels)]
            self.out_sem = out_l.at[where]
            self.plan(order_of(kind, levels))

        def plan(self, order):
            self.moves, self.backs = [], []
            base, size, block_list, landing, sem = 0, self.depth, [0, 1], 0, 0
            for step in order:
                move = []
                if step == "y":
                    device, sent, kept, from_blocks, block_list = (r, far), base, base, [1], [0]
                else:
                    size //= 2
                    side = (r // 2**step) % 2
                    device, sent, kept, from_blocks = (
                        peers[step], base + (1 - side) * size, base + side * size, block_list,
                    )
                    self.backs.append((device, part(kept, size)))
                for k, block in enumerate(from_blocks):
                    move.append(
                        (device, block, part(sent, size), block_list[k], part(kept, size),
                         pl.ds(landing, size), self.rs_sems[sem])
                    )
                    landing += size
                    sem += 1
                self.moves.append(move)
                base = kept
            self.backs.reverse()

        def core_copies(self):
            return [
                remote(self.grads.at[b], self.core.at[k], *self.core_sems[k], (r, core))
                for k, b in enumerate((core, both))
            ]

        def rs_copies(self, i):
            return [
                remote(self.total.at[block, sent], self.land.at[landing], *sems, device)
                for device, block, sent, _, _, landing, sems in self.moves[i]
            ]

        def add(self, i):
            for _, _, _, block, kept, landing, _ in self.moves[i]:
                self.total[block, kept] += self.land[landing]

        def ag_copy(self, i):
            device, kept = self.backs[i]
            dst = self.out.at[kept]
            return remote(self.total.at[0, kept] if i == 0 else dst, dst, *self.ag_sems[i], device)

        def out_local(self):
            kept = self.backs[0][1]
            return pltpu.make_async_copy(self.total.at[0, kept], self.out.at[kept], self.out_sem)

    class HeadUnit(Unit):
        def __init__(self):
            self.depth = h_grads.shape[1]
            self.grads, self.core, self.total, self.land, self.out = h_grads, h_core, h_total, h_land, ghead_out
            sems = [(hu_s.at[k], hu_r.at[k]) for k in range(2 * levels + 4)]
            self.core_sems, self.rs_sems, self.ag_sems = sems[:2], sems[2 : levels + 4], sems[levels + 4 :]
            self.out_sem = hu_l.at[0]
            self.plan(order_of("A", levels))

    def stage_core(unit):
        wait(unit.core_copies())
        unit.total[1] = unit.grads[far] + unit.core[1]
        unit.total[0] = unit.grads[f] + unit.core[0]
        start(unit.rs_copies(0))

    def stage_sum(i, unit):
        wait(unit.rs_copies(i))
        unit.add(i)
        if i < levels:
            start(unit.rs_copies(i + 1))
        else:
            unit.ag_copy(0).start()
            unit.out_local().start()

    def stage_out(i, unit):
        if i == 0:
            unit.out_local().wait()
        unit.ag_copy(i).wait()
        if i + 1 < levels:
            unit.ag_copy(i + 1).start()

    stages = [stage_core]
    stages += [functools.partial(stage_sum, i) for i in range(levels + 1)]
    stages += [functools.partial(stage_out, i) for i in range(levels)]

    def outer(m, u, right):
        for t in range(2):
            tile = split(right[:, t * half : (t + 1) * half])
            tile = dot3((upper[0], upper[1]), tile, TN)
            for b in range(half // LANES):
                grads[u % 2, t * (half // LANES) + b] = tile[:, b * LANES : (b + 1) * LANES]

    def back(m, left, t):
        return dot3(left, split(weight[which[m], t * half : (t + 1) * half, :]), NT)

    def compute(step, m, ready):
        s = sections - 1 - step
        u = 3 * step + m
        wait(w_load(s, which[m]))
        h = hs[s]
        if m == 0:
            z, reset, c = zs[s], rs[s], cs[s]
            put(reset * h, low_cols)
            put(x_buf[...] * par[pl.ds(s, 1), :], high_cols)
            d_out = dh[...] * z * (1.0 - c * c)
            vec[pl.ds(2 * sections + s, 1), :] = jnp.sum(d_out, axis=0, keepdims=True)
            outer(m, u, d_out)
            ready()
            left = split(d_out)
            for t in range(4):
                d_in[:, t * half : (t + 1) * half] = back(m, left, t)
            d_reset[...] = d_in[:, 0:width] * h * reset * (1.0 - reset)
        elif m == 1:
            z, reset, c = zs[s], rs[s], cs[s]
            put(h, low_cols)
            d_up = dh[...] * (c - h) * z * (1.0 - z)
            vec[pl.ds(s, 1), :] = jnp.sum(d_up, axis=0, keepdims=True)
            outer(m, u, d_up)
            ready()
            dh[...] = dh[...] * (1.0 - z) + d_in[:, 0:width] * reset
            left = split(d_up)
            for t in range(4):
                cols = slice(t % 2 * half, (t % 2 + 1) * half)
                if t < 2:
                    dh[:, cols] += back(m, left, t)
                else:
                    d_in[:, t * half : (t + 1) * half] += back(m, left, t)
        else:
            d_r = d_reset[...]
            vec[pl.ds(sections + s, 1), :] = jnp.sum(d_r, axis=0, keepdims=True)
            outer(m, u, d_r)
            ready()
            left = split(d_r)
            for t in range(4):
                cols = slice(t % 2 * half, (t % 2 + 1) * half)
                if t < 2:
                    dh[:, cols] += back(m, left, t)
                else:
                    d_xs = d_in[:, t * half : (t + 1) * half] + back(m, left, t)
                    gin[:, cols] += d_xs * par[pl.ds(s, 1), cols]
                    vec[pl.ds(3 * sections + s, 1), cols] = jnp.sum(d_xs * x_buf[:, cols], axis=0, keepdims=True)

        @pl.when(step + 1 < sections)
        def _():
            start(w_load(s - 1, which[m]))

    gf_copies = [
        remote(gin.at[:, lanes(peer)], gfeat_out.at[own_rows], gf_s.at[k], gf_r.at[k], (r, peer))
        for k, peer in enumerate(others)
    ]
    gf_local = pltpu.make_async_copy(gin.at[:, lanes(f)], gfeat_out.at[own_rows], gf_l.at[0])
    vec_feat = [
        remote(ex_c.at[peer], ex_c_feat.at[f], ef_s.at[2, k], ef_r.at[2, k], (r, peer)) for k, peer in enumerate(others)
    ]
    vec_rows = rows_step(2, ex_c_mid, ex_c_rows)
    vec_last = feat_step(3, ex_d, ex_d_feat)
    spread = hid // LANES

    sums, _ = sum_all(1, sums, ex_b, ex_b_feat, ex_b_rows, sum_slots, head_rest)
    g_gain, g_shift = unstack(sums[0:blocks]), unstack(sums[blocks:])
    dh[...] = inv_std * (dh[...] * gain - column / count * gain * (g_shift + x_hat[...] * g_gain))
    tiny_out[...] = sums
    gin[...] = jnp.zeros_like(gin)

    def before(step, j, back_by):
        u = j - back_by
        return step + u // slots, u % slots

    delays = schedule(levels)

    @pl.loop(0, sections + -(-delays[-1] // slots))
    def _(step):
        for j in range(slots):

            @pl.when(step < sections)
            def _():
                def ready():
                    start(Unit(step, j).core_copies())

                if j % cuts == 0:
                    compute(step, j // cuts, ready)
                else:
                    ready()

            for delay, stage in zip(delays, stages, strict=True):
                s1, j1 = before(step, j, delay)
                if j1 == slots - 1:

                    @pl.when(s1 == -1)
                    def _():
                        stage(HeadUnit())

                groups = (s1 == 0, (s1 > 0) & (s1 < sections - 1), s1 == sections - 1)
                for kind in sorted({row[j1] for row in kinds}):
                    active = [g for g, row in zip(groups, kinds, strict=True) if row[j1] == kind]

                    @pl.when(functools.reduce(jnp.logical_or, active))
                    def _():
                        stage(Unit(s1, j1, kind))

            if j == 0:

                @pl.when(step == sections)
                def _():
                    for b in range(blocks):
                        ex_c[b, 0:aux] = vec[0:aux, b * LANES : (b + 1) * LANES]
                        ex_c[b, aux : aux + 8] = vec[
                            aux + 8 * (b // spread) : aux + 8 * (b // spread + 1),
                            LANES * (b % spread) : LANES * (b % spread + 1),
                        ]
                    ex_c_feat[f] = ex_c[f]
                    start(vec_feat)
                    gin[...] += dh[...]
                    start(gf_copies + [gf_local])

            if j == 2:

                @pl.when(step == sections)
                def _():
                    wait(vec_feat)
                    ex_c_mid[...] = sum_slots(ex_c_feat)
                    ex_c_rows[r] = ex_c_mid[...]
                    start(vec_rows)

            if j == 5:

                @pl.when(step == sections)
                def _():
                    wait(vec_rows)
                    sums = sum_slots(ex_c_rows)
                    own_out[...] = sums[0:aux]
                    scale = par[0:sections, lanes(f)]
                    inner = jnp.sum(scale * sums[3 * sections : aux], axis=1, keepdims=True) / width
                    ex_d[...] = jnp.zeros_like(ex_d)
                    ex_d[0:sections] = jnp.broadcast_to(inner, (sections, LANES))
                    ex_d[8:16] = sums[aux : aux + 8]
                    ex_d_feat[f] = ex_d[...]
                    start(vec_last)

    wait(vec_last)
    inner = sum_slots(ex_d_feat)[0:sections]
    own_out[3 * sections : aux] = par[0:sections, lanes(f)] * (own_out[3 * sections : aux] - inner)
    for b in range(blocks):
        aux_out[8 * (b // spread) : 8 * (b // spread + 1), LANES * (b % spread) : LANES * (b % spread + 1)] = (
            ex_d_feat[b, 8:16]
        )
    wait(gf_copies + [gf_local])
    wait(logit_copies)
    for b in range(blocks):
        logit_out[:, b * mine : (b + 1) * mine] = logit_buf[b]

    @pl.loop(0, sections)
    def _(s):
        for m in range(3):
            for copy in (y_copy, own_copy, x_copy, z_copy, far_copy):
                copy(s, m).wait_send()

    @pl.loop(0, final)
    def _(s):
        for m in range(3):
            for copy in (a_copy, b_copy, c_copy):
                copy(s, m).wait_send()

    for m in range(3):
        a_copy(final, m, True).wait_send()

    for copy in firsts + heads + unsent:
        copy.wait_send()


def finish_kernel(
    sections, classes,
    gz_ref, gr_ref, go_ref, gfeat_ref, ghead_ref, logit_ref, tiny_ref, own_ref, aux_ref,
    logit_out, gfeat_out, gmask_out, gz_out, gr_out, go_out, bz_out, br_out, bo_out,
    gain_out, shift_out, ghead_out, bhead_out, wout_out, bout_out,
    store,
):
    f = lax.axis_index("feat")
    pairs = [(gfeat_ref, gfeat_out)] + [
        (src.at[s], dst.at[s])
        for s in range(sections)
        for src, dst in ((gz_ref, gz_out), (gr_ref, gr_out), (go_ref, go_out))
    ]
    stores = [pltpu.make_async_copy(src, dst, store.at[k]) for k, (src, dst) in enumerate(pairs)]
    for copy in stores:
        copy.start()
    block = gfeat_ref.shape[1]
    hidden = bhead_out.shape[1]
    logit_out[...] = logit_ref[0:classes]
    for k, out in enumerate((bz_out, br_out, bo_out, gmask_out)):
        out[...] = own_ref[k * sections : (k + 1) * sections]
    gain_out[...] = tiny_ref[pl.ds(f, 1)]
    shift_out[...] = tiny_ref[pl.ds(tiny_ref.shape[0] // 2 + f, 1)]
    for t in range(hidden // block):
        ghead_out[:, t * block : (t + 1) * block] = ghead_ref[t * block : (t + 1) * block]
    wout_out[...] = aux_ref[0:classes]
    bhead_out[...] = aux_ref[classes : classes + 1]
    bout_out[...] = aux_ref[classes + 1 : classes + 2, 0:classes]
    for copy in stores:
        copy.wait()


def layer(
    rows, groups, features, w_update, w_reset, w_candidate, w_head, counts, validity, mask_logits, b_update, b_reset,
    b_candidate, norm_gain, norm_shift, b_head, w_out, b_out, cotangent,
):
    sections, depth, block = w_update.shape
    width, mine = groups * block, features.shape[0] // groups
    hidden = w_head.shape[1]
    classes = w_out.shape[0]
    units = 3 * sections
    levels = rows.bit_length() - 1
    head_depth = max(hidden, 8 * rows)
    cuts = cuts_of(levels)
    slots = 3 * cuts
    piece = depth // cuts
    held, landed = rings(levels)
    long = 4 * sections + TALL
    sds = jax.ShapeDtypeStruct
    dma = pltpu.SemaphoreType.DMA
    any_, vmem = pl.BlockSpec(memory_space=pl.ANY), pl.BlockSpec(memory_space=pltpu.VMEM)
    grad = sds((sections, depth, block), F32)
    held_grad = pltpu.VMEM((sections, depth, block), F32)

    def buf(*shape):
        return pltpu.VMEM(shape, F32)

    made = pl.pallas_call(
        functools.partial(kernel, sections, rows, levels, classes),
        out_shape=[
            held_grad, held_grad, held_grad,
            pltpu.VMEM(features.shape, F32),
            pltpu.VMEM((head_depth, block), F32),
            pltpu.VMEM((TALL, groups * mine), F32),
            pltpu.VMEM((2 * groups, block), F32),
            pltpu.VMEM((4 * sections, block), F32),
            pltpu.VMEM((TALL, hidden), F32),
            sds((sections, 3, groups, depth, block), F32),
        ],
        in_specs=[any_] * 5 + [pl.BlockSpec(memory_space=pltpu.SMEM)] + [vmem] * 11,
        out_specs=[vmem] * 9 + [any_],
        scratch_shapes=[
            buf(mine, width), buf(groups, PAR, block), buf(PAR, width), buf(sections + 1, mine, width),
            buf(sections, mine, width), buf(sections, mine, width), buf(sections, mine, width),
            buf(3, depth, width), pltpu.VMEM((2, mine, depth), BF16),
            buf(width, hidden), buf(mine, width), buf(groups, TALL, mine), buf(mine, width),
            buf(mine, depth), buf(mine, width), buf(mine, width), buf(long, width),
            buf(PAR, block), buf(TALL, hidden), buf(TALL, mine), buf(8, LANES),
            buf(2, groups, depth, block), buf(slots, 2, piece, block), buf(held, slots, 2, piece, block),
            buf(landed, slots, 2 * piece, block),
            buf(groups, head_depth, block), buf(2, head_depth, block), buf(2, head_depth, block),
            buf(2 * head_depth, block),
            buf(2, 16, LANES), buf(groups, 16, LANES), buf(rows, 16, LANES),
            buf(2, 2 * groups, LANES), buf(groups, 2 * groups, LANES), buf(rows, 2 * groups, LANES),
            buf(groups, 4 * sections + 8, block), buf(groups, 4 * sections + 8, block), buf(4 * sections + 8, block),
            buf(rows, 4 * sections + 8, block), buf(16, block), buf(groups, 16, block),
            dma((9,)), dma((9,)), dma((3,)),
        ] + [dma((units,))] * 16 + [
            dma((3, groups)), dma((3,)), dma((3,)), dma((3,)), dma((3,)), dma((1,)),
            dma((4, 3)), dma((4, 3)), dma((3, rows - 1)), dma((3, rows - 1)),
            dma((2, slots)), dma((2, slots)), dma((levels + 2, landed, slots)), dma((levels + 2, landed, slots)),
            dma((levels, 3 * slots)), dma((levels, 3 * slots)), dma((3 * slots,)),
            dma((2 * levels + 4,)), dma((2 * levels + 4,)), dma((1,)),
        ],
        compiler_params=pltpu.CompilerParams(
            collective_id=0, has_side_effects=True, vmem_limit_bytes=52 * 2**20
        ),
    )(
        features, w_update, w_reset, w_candidate, w_head, counts, validity[None], mask_logits, b_update, b_reset,
        b_candidate, norm_gain[None], norm_shift[None], b_head[None], w_out, b_out[None], cotangent,
    )
    row = sds((1, block), F32)
    bias = sds((sections, block), F32)
    return pl.pallas_call(
        functools.partial(finish_kernel, sections, classes),
        out_shape=[
            sds((classes, groups * mine), F32), sds(features.shape, F32), bias, grad, grad, grad, bias, bias, bias,
            row, row, sds((block, hidden), F32), sds((1, hidden), F32), sds((classes, hidden), F32),
            sds((1, classes), F32),
        ],
        in_specs=[vmem] * 3 + [vmem] + [vmem] * 5,
        out_specs=[vmem, any_, vmem, any_, any_, any_] + [vmem] * 9,
        scratch_shapes=[dma((units + 1,))],
        compiler_params=pltpu.CompilerParams(vmem_limit_bytes=16 * 2**20),
    )(*made[:9])


def local(
    rows, groups, features, counts, validity, mask_logits, w_update, w_reset, w_candidate, b_update, b_reset,
    b_candidate, norm_gain, norm_shift, w_head, b_head, w_out, b_out, cotangent,
):
    out = layer(
        rows, groups, features, w_update, w_reset, w_candidate, w_head, counts, validity, mask_logits, b_update,
        b_reset, b_candidate, norm_gain, norm_shift, b_head, w_out.T, b_out, cotangent.T,
    )
    logits, g_feat, g_mask, gz, gr, go, bz, br, bo, gain, shift, g_head, g_b_head, g_w_out, g_b_out = out
    return (
        logits.T, g_feat, g_mask, gz, gr, go, bz, br, bo, gain[0], shift[0], g_head, g_b_head[0], g_w_out.T,
        g_b_out[0],
    )


def solution(mesh):
    rows, groups = mesh.shape["rows"], mesh.shape["feat"]
    split_cols, by_feat = P(None, None, "feat"), P("feat")
    return jax.shard_map(
        functools.partial(local, rows, groups),
        mesh=mesh,
        in_specs=(
            P("rows", "feat"), P("rows"), P("rows"), P(None, "feat"), split_cols, split_cols, split_cols,
            P(None, "feat"), P(None, "feat"), P(None, "feat"), by_feat, by_feat, P("feat", None),
            P(), P(), P(), P("rows", None),
        ),
        out_specs=(
            P("rows", None), P("rows", "feat"), P(None, "feat"), split_cols, split_cols, split_cols,
            P(None, "feat"), P(None, "feat"), P(None, "feat"), by_feat, by_feat, P("feat", None),
            P(), P(), P(),
        ),
        check_vma=False,
    )
```
